512 devices in a mesh: dp: 32 (over x, z), group: 16 (over y, core).
Axes of the slice: x: 4, y: 8, z: 8, core: 2. Of those that a mesh axis runs over, the one named last changes fastest.
Arguments:
- queries: bfloat16 [24576, 4096], P('dp', 'group'), may hold values from -120 to 120
- passages: bfloat16 [24576, 4096], P('dp', 'group'), may hold values from -120 to 120
- neg_owner: int32 [24576, 8], P('dp'), may hold values from 0 to 31, all different within a row; in each aligned block of 768 rows (0 to 767, 768 to 1535, ...) at most 240 rows name the same one
- neg_row: int32 [24576, 8], P('dp'), may hold values from 0 to 767
- gain: float32 [4096], replicated, may hold values from 0.5 to 1.5
Outputs:
- grad_queries: bfloat16 [24576, 4096], P('dp', 'group')
- grad_passages: bfloat16 [24576, 4096], P('dp', 'group')
- grad_gain: float32 [4096], replicated
- loss: float32 [], replicated
The draws below stay inside these ranges and needn't reach their ends.
Inputs may be any that keep to these rules, and one draw needn't show every extreme that they name: `neg_owner`: the 8 owners of one query are distinct; among the 768 queries of one data group no owner is named more than 240 times, and that many in every draw.
All inputs are finite; a program needn't handle non-finite values.
Results may differ from the reference program's by a relative error of at most 0.00305.
The reference program's roundings to bfloat16 on the way count: a program that leaves them out, or rounds other values in their place, can miss the bound.
Values may be sent and summed in bfloat16 or wider, within the bound.
No kernel may reach another device: no remote copies, remote signals or barrier semaphores. Data moves between devices by JAX's collectives and lax.ppermute only.
A program may use at most 64 MiB of HBM per device.

```python
import math
import jax
import jax.numpy as jnp
import numpy as np
from jax import lax

VECTOR_LENGTH = 4096
BATCH = 768
NEG = 8
CAP = 240
QUERIES = 24576
N_DP = 32


def common_direction(key):
    return jax.random.uniform(jax.random.fold_in(key, 31), (1, VECTOR_LENGTH), jnp.float32, -1.7, 1.7)


def passage_rows(key, direction, fraction):
    normal_part = jnp.clip(jax.random.normal(jax.random.fold_in(key, 21), (QUERIES, VECTOR_LENGTH), jnp.float32), -4.0, 4.0)
    rough = normal_part
    rough = jnp.sqrt(fraction) * direction + jnp.sqrt(1.0 - fraction) * rough
    row_scale = jnp.exp(jax.random.uniform(jax.random.fold_in(key, 23), (QUERIES, 1), jnp.float32, 0.0, math.log(10.0)))
    col_scale = jnp.exp(jax.random.uniform(jax.random.fold_in(key, 24), (1, VECTOR_LENGTH), jnp.float32, 0.0, math.log(3.0)))
    values = rough * row_scale * col_scale
    placed = (jnp.arange(QUERIES) % BATCH == 8)[:, None]
    return jnp.where(placed, values, values)


def draw_passages(key, part):
    passage_share = 0.0
    direction = common_direction(key)
    return passage_rows(key, direction, passage_share).astype(jnp.bfloat16)


def draw_queries(key, part):
    query_share = 0.0
    direction = common_direction(key)
    key = jax.random.fold_in(key, 3)
    fraction = query_share * jax.random.uniform(jax.random.fold_in(key, 41), (QUERIES, 1), jnp.float32)
    private = passage_rows(key, direction, fraction)
    placed = (jnp.arange(QUERIES) % BATCH == 3)[:, None]
    aligned = private
    return jnp.where(placed, aligned, private).astype(jnp.bfloat16)


def plant(values, key, low, top_value):
    longest = values.shape.index(max(values.shape))
    spots = []
    for shift in (0, 1):
        where = [jax.random.randint(jax.random.fold_in(key, axis), (), 0, length) for axis, length in enumerate(values.shape)]
        where[longest] = (where[longest] + shift) % values.shape[longest]
        spots.append(tuple(where))
    return values.at[spots[0]].set(low).at[spots[1]].set(top_value)


def rank_table(count, skew):
    weights = [(1 << 20) // math.isqrt(grade ** skew) + 1 for grade in range(1, count + 1)]
    scale = 1 + sum(weights) // (1 << 30)
    return np.cumsum(np.array([max(1, weight // scale) for weight in weights]))


def skewed_ids(key, extent, count, lean):
    table = rank_table(count, lean)
    lot = jax.random.randint(jax.random.fold_in(key, 1), extent, 0, int(table[count - 1]))
    grade = jnp.searchsorted(jnp.asarray(table, jnp.int32), lot, side="right")
    return jax.random.permutation(jax.random.fold_in(key, 2), count)[grade].astype(jnp.int32)


def assign_block(key, own, number, rows, amount, top, bound, skew):
    sequence = jax.random.permutation(key, amount)
    crowded, ordinary = shares(amount, rows * top, bound, skew, True), shares(amount, rows * top, bound, skew, False)
    places = jnp.arange(amount)

    def named(tallies, rotation):
        used = int((tallies > 0).sum())
        fixed = max(1, used // 4)
        passed = fixed + (places - fixed + rotation * (used - fixed)) % max(1, amount - fixed)
        return jnp.zeros((amount,), jnp.int32).at[sequence[jnp.where(places < fixed, places, passed)]].set(jnp.asarray(tallies, jnp.int32))

    tallies = jnp.where(number % 4 == 0, named(crowded, number // 4), named(ordinary, number - number // 4 - 1))
    mixed = jax.random.permutation(jax.random.fold_in(own, 3), amount)
    giver, receiver = mixed[0:amount // 2 * 2:2], mixed[1:amount // 2 * 2:2]
    margin = jnp.minimum(tallies[giver] - 1, bound - tallies[receiver]) // 2
    margin = jnp.where((giver == sequence[0]) | (receiver == sequence[0]) | (tallies[receiver] == 0), 0, jnp.maximum(margin, 0))
    passed = jax.random.randint(jax.random.fold_in(own, 4), (amount // 2,), 0, 1 << 20) % (margin + 1)
    tallies = tallies.at[giver].add(-passed).at[receiver].add(passed)
    items = jnp.searchsorted(jnp.cumsum(tallies), jnp.arange(rows * top), side="right").astype(jnp.int32)
    table = items.reshape(top, rows).T
    table = table[jax.random.permutation(jax.random.fold_in(own, 1), rows)]
    rotation = jax.random.randint(jax.random.fold_in(own, 2), (rows, 1), 0, top)
    return jnp.take_along_axis(table, (jnp.arange(top)[None, :] + rotation) % top, axis=1)


def shares(amount, total, limit, lean, full):
    portions = [(1 << 20) // math.isqrt(standing ** lean) + 1 for standing in range(1, amount + 1)]
    largest = limit if full else min(limit, max(-(-total // amount), total * portions[0] // sum(portions)))
    least = 1 if total - largest >= amount - 1 else 0
    holding, rest = [largest] + [least] * (amount - 1), total - largest - least * (amount - 1)
    while rest > 0:
        free = [i for i in range(1, amount) if holding[i] < largest] or [i for i in range(1, amount) if holding[i] < limit]
        pool, remaining = sum([portions[i] for i in free]), rest
        for i in free:
            more = min(limit - holding[i], max(1, remaining * portions[i] // pool), rest)
            holding[i] = holding[i] + more
            rest = rest - more
    return np.array(holding)


def setup_inputs(seed: int = 0) -> dict:
    streams_of = jax.random.split(jax.random.key(seed), 6)
    queries = draw_queries(jax.random.fold_in(streams_of[5], 71), 0)
    passages = draw_passages(jax.random.fold_in(streams_of[5], 71), 0)
    neg_owner_keys = jax.random.split(jax.random.fold_in(streams_of[2], 1), QUERIES // BATCH)
    neg_owner_turns = jax.random.permutation(jax.random.fold_in(streams_of[2], 3), QUERIES // BATCH)
    neg_owner = jax.vmap(lambda own, number: assign_block(jax.random.fold_in(streams_of[2], 2), own, number, BATCH, N_DP, NEG, CAP, 2))(neg_owner_keys, neg_owner_turns).reshape((QUERIES, NEG))
    neg_row = plant(skewed_ids(streams_of[3], (QUERIES, NEG), BATCH, 2), jax.random.fold_in(streams_of[3], 3), 0, BATCH - 1).astype(jnp.int32)
    gain = jnp.clip(1.0 + 0.1 * jax.random.normal(streams_of[4], (VECTOR_LENGTH,), jnp.float32), 0.5, 1.5)
    return {"queries": queries, "passages": passages, "neg_owner": neg_owner, "neg_row": neg_row, "gain": gain}


EPSILON = 1e-06
SOFTNESS_DIVISOR = 0.25

def embed(rows, gain):
    values = rows.astype(jnp.float32)
    inverse = lax.rsqrt(lax.optimization_barrier(jnp.mean(values * values, axis=1, keepdims=True)) + EPSILON)
    normed = values * inverse
    return ((normed * gain).astype(jnp.bfloat16), normed, inverse)

def norm_back(grad_emb, normed, inverse, gain):
    inner = grad_emb * gain
    return inverse * (inner - normed * lax.optimization_barrier(jnp.mean(inner * normed, axis=1, keepdims=True)))

def reference(queries, passages, neg_owner, neg_row, gain):
    multiplier_coefficient = 1.0 / (SOFTNESS_DIVISOR * math.sqrt(VECTOR_LENGTH))
    q_emb, q_normed, q_inverse = embed(queries, gain)
    p_emb, p_normed, document_reciprocal_norm = embed(passages, gain)
    neg_ids = (neg_owner * BATCH + neg_row).astype(jnp.int32)

    def block(carry, index):
        start = (index * BATCH).astype(jnp.int32)
        q_blk = lax.dynamic_slice_in_dim(q_emb, start, BATCH, 0)
        p_blk = lax.dynamic_slice_in_dim(p_emb, start, BATCH, 0)
        id_blk = lax.dynamic_slice_in_dim(neg_ids, start, BATCH, 0)
        hard = jnp.take(p_emb, id_blk.reshape(-1), axis=0).reshape(BATCH, NEG, VECTOR_LENGTH)
        scores = jnp.dot(q_blk, p_blk.T, preferred_element_type=jnp.float32) * multiplier_coefficient
        near = jnp.einsum('qd,qkd->qk', q_blk.astype(jnp.float32), hard.astype(jnp.float32)) * multiplier_coefficient
        top = jnp.maximum(lax.optimization_barrier(jnp.max(scores, axis=1)), lax.optimization_barrier(jnp.max(near, axis=1)))[:, None]
        total = lax.optimization_barrier(jnp.sum(jnp.exp(scores - top), axis=1, keepdims=True)) + lax.optimization_barrier(jnp.sum(jnp.exp(near - top), axis=1, keepdims=True))
        lse = top + jnp.log(total)
        losses = lse[:, 0] - jnp.diagonal(scores)
        eye = jnp.eye(BATCH, dtype=jnp.float32)
        weights = (jnp.exp(scores - lse) - eye).astype(jnp.bfloat16)
        hard_weights = jnp.exp(near - lse).astype(jnp.bfloat16)
        grad_q = (jnp.dot(weights, p_blk, preferred_element_type=jnp.float32) + jnp.einsum('qk,qkd->qd', hard_weights.astype(jnp.float32), hard.astype(jnp.float32))) * multiplier_coefficient
        grad_p = jnp.dot(weights.T, q_blk, preferred_element_type=jnp.float32) * multiplier_coefficient
        pair = ((hard_weights.astype(jnp.float32) * multiplier_coefficient)[:, :, None] * q_blk.astype(jnp.float32)[:, None, :]).astype(jnp.bfloat16)
        carry = carry.at[id_blk.reshape(-1)].add(pair.reshape(-1, VECTOR_LENGTH).astype(jnp.float32))
        return (carry, (grad_q, grad_p, losses))
    hard_total, (grad_q, grad_p, losses) = lax.scan(block, jnp.zeros((QUERIES, VECTOR_LENGTH), jnp.float32), jnp.arange(N_DP, dtype=jnp.int32))
    grad_q = grad_q.reshape(QUERIES, VECTOR_LENGTH)
    grad_p = grad_p.reshape(QUERIES, VECTOR_LENGTH) + hard_total
    grad_queries = norm_back(grad_q, q_normed, q_inverse, gain).astype(jnp.bfloat16)
    grad_passages = norm_back(grad_p, p_normed, document_reciprocal_norm, gain).astype(jnp.bfloat16)
    grad_gain = (lax.optimization_barrier(jnp.sum(grad_q * q_normed, axis=0)) + lax.optimization_barrier(jnp.sum(grad_p * p_normed, axis=0))) / math.sqrt(QUERIES)
    loss = jnp.sum(losses) / QUERIES
    return (grad_queries, grad_passages, grad_gain, loss)
```

```python
import functools
import math

import jax
import jax.numpy as jnp
from jax import lax
from jax.experimental import pallas as pl
from jax.experimental.pallas import tpu as pltpu
from jax.sharding import PartitionSpec as P

EPSILON = 1e-06
SOFTNESS_DIVISOR = 0.25
ABSENT = -1e30
F32 = jnp.float32
BF16 = jnp.bfloat16


def iota(shape, axis):
    return lax.broadcasted_iota(jnp.int32, shape, axis)


def contract(a, b, da, db):
    return lax.dot_general(a, b, (((da,), (db,)), ((), ())), preferred_element_type=F32)


def call(kernel, grid, in_specs, out_specs, out_shape, flops, bytes_accessed, scratch=()):
    return pl.pallas_call(
        kernel,
        grid=(grid,),
        in_specs=in_specs,
        out_specs=out_specs,
        out_shape=out_shape,
        scratch_shapes=list(scratch),
        compiler_params=pltpu.CompilerParams(vmem_limit_bytes=24 * 1024 * 1024),
        cost_estimate=pl.CostEstimate(flops=flops, bytes_accessed=bytes_accessed, transcendentals=0),
    )


def whole(shape):
    return pl.BlockSpec(shape, lambda i: (0,) * len(shape))


def slab(cap, piece):
    return pl.BlockSpec((1, cap, piece), lambda i: (i, 0, 0))


def slots_kernel(cap, owner_ref, row_ref, q_ref, pos_ref, rows_ref, column_ref, slot_ref, asked_ref):
    step = pl.program_id(0)
    negs, rows = owner_ref.shape
    n_data = pos_ref.shape[0]

    @pl.when(step == 0)
    def _():
        ids = iota((n_data, rows), 0)
        asked = jnp.full((n_data, rows), -1, jnp.int32)
        for k in range(negs):
            asked = jnp.where(owner_ref[k : k + 1, :] == ids, row_ref[k : k + 1, :], asked)
        hit = jnp.where(asked >= 0, 1.0, 0.0).astype(BF16)
        before = jnp.where(iota((rows, rows), 0) < iota((rows, rows), 1), 1.0, 0.0).astype(BF16)
        count = contract(hit, before, 1, 0)
        pos_ref[...] = jnp.where(asked >= 0, count.astype(jnp.int32), -1)
        asked_ref[...] = asked
        column_ref[...] = jnp.zeros_like(column_ref)

    pick = jnp.where(iota((cap, rows), 0) == pos_ref[pl.ds(step, 1), :], 1.0, 0.0).astype(BF16)
    slot_ref[0] = contract(pick, q_ref[...], 1, 0).astype(BF16)
    code = asked_ref[pl.ds(step, 1), :] + 1
    part = iota((8, rows), 0)
    digits = jnp.where(part == 0, code >> 5, jnp.where(part == 1, code & 31, 0))
    digits = digits.astype(F32).astype(BF16)
    found = contract(digits, pick, 1, 1)
    rows_ref[0] = found[0:1, :] * 32.0 + found[1:2, :] - 1.0
    column = contract(pick, digits, 1, 1)
    column = column[:, 0:1] * 32.0 + column[:, 1:2] - 1.0
    column_ref[...] += jnp.where(iota(column_ref.shape, 1) == step, column, 0.0)


def make_slots(owner_t, row_t, q_emb, n_data, cap):
    negs, rows = owner_t.shape
    piece = q_emb.shape[1]
    return call(
        functools.partial(slots_kernel, cap),
        n_data,
        [whole((negs, rows)), whole((negs, rows)), whole((rows, piece))],
        [
            whole((n_data, rows)),
            pl.BlockSpec((1, 1, cap), lambda i: (i, 0, 0)),
            whole((cap, n_data)),
            slab(cap, piece),
        ],
        [
            jax.ShapeDtypeStruct((n_data, rows), jnp.int32),
            jax.ShapeDtypeStruct((n_data, 1, cap), F32),
            jax.ShapeDtypeStruct((cap, n_data), F32),
            jax.ShapeDtypeStruct((n_data, cap, piece), BF16),
        ],
        2 * n_data * cap * rows * piece,
        n_data * cap * piece * 2,
        [pltpu.VMEM((n_data, rows), jnp.int32)],
    )(owner_t, row_t, q_emb)


def near_kernel(scale, pos_ref, column_ref, inverse_ref, gain_ref, q_ref, p_ref, slot_ref, near_ref):
    step = pl.program_id(0)
    cap = q_ref.shape[1]
    rows = p_ref.shape[0]
    column = jnp.sum(
        jnp.where(iota(column_ref.shape, 1) == step, column_ref[...], 0.0), axis=1, keepdims=True
    ).astype(jnp.int32)
    match = iota((cap, rows), 1) == column
    raw = contract(jnp.where(match, 1.0, 0.0).astype(BF16), p_ref[...], 1, 0)
    inverse = jnp.sum(jnp.where(match, inverse_ref[pl.ds(step, 1), :], 0.0), axis=1, keepdims=True)
    emb = ((raw * inverse) * gain_ref[...]).astype(BF16)
    slot_ref[0] = emb
    score = jnp.sum(q_ref[0].astype(F32) * emb.astype(F32), axis=1, keepdims=True) * scale
    pos = pos_ref[pl.ds(step, 1), :]
    spread = jnp.sum(jnp.where(iota((cap, rows), 0) == pos, score, 0.0), axis=0, keepdims=True)
    near_ref[pl.ds(step, 1), :] = jnp.where(pos >= 0, spread, ABSENT)


def near_scores(scale, pos, column, inverse_all, gain, q_slots, p_all):
    n_data, cap, piece = q_slots.shape
    rows = pos.shape[1]
    return call(
        functools.partial(near_kernel, scale),
        n_data,
        [
            whole((n_data, rows)),
            whole((cap, n_data)),
            whole((n_data, rows)),
            whole((1, piece)),
            slab(cap, piece),
            pl.BlockSpec((rows, piece), lambda i: (i, 0)),
        ],
        [slab(cap, piece), whole((n_data, rows))],
        [
            jax.ShapeDtypeStruct((n_data, cap, piece), BF16),
            jax.ShapeDtypeStruct((n_data, rows), F32),
        ],
        2 * n_data * cap * rows * piece,
        n_data * rows * piece * 2,
    )(pos, column, inverse_all, gain, q_slots, p_all)


def softmax_kernel(first_ref, scores_ref, near_ref, weights_ref, hard_ref, loss_ref):
    scores = jnp.sum(scores_ref[...], axis=0)
    near = near_ref[...]
    top = jnp.maximum(jnp.max(scores, axis=1, keepdims=True), jnp.max(near, axis=1, keepdims=True))
    total = jnp.sum(jnp.exp(scores - top), axis=1, keepdims=True) + jnp.sum(
        jnp.exp(near - top), axis=1, keepdims=True
    )
    lse = top + jnp.log(total)
    positive = iota(scores.shape, 1) == iota(scores.shape, 0) + first_ref[0]
    diagonal = jnp.sum(jnp.where(positive, scores, 0.0), axis=1, keepdims=True)
    weights_ref[...] = (jnp.exp(scores - lse) - jnp.where(positive, 1.0, 0.0)).astype(BF16)
    hard_ref[...] = jnp.exp(near - lse).astype(BF16)
    loss_ref[...] = jnp.sum(lse - diagonal, axis=0, keepdims=True)


def softmax_share(first, scores, near):
    parts, share, rows = scores.shape
    n_data = near.shape[1]
    return call(
        softmax_kernel,
        1,
        [pl.BlockSpec(memory_space=pltpu.SMEM), whole((parts, share, rows)), whole((share, n_data))],
        [whole((share, rows)), whole((share, n_data)), whole((1, 1))],
        [
            jax.ShapeDtypeStruct((share, rows), BF16),
            jax.ShapeDtypeStruct((share, n_data), BF16),
            jax.ShapeDtypeStruct((1, 1), F32),
        ],
        8 * share * rows,
        parts * share * rows * 4,
    )(first, scores, near)


def weigh_kernel(pos_ref, hard_ref, table_ref):
    step = pl.program_id(0)
    cap = table_ref.shape[0]
    rows = pos_ref.shape[1]

    @pl.when(step == 0)
    def _():
        table_ref[...] = jnp.zeros_like(table_ref)

    match = iota((cap, rows), 0) == pos_ref[pl.ds(step, 1), :]
    column = jnp.sum(jnp.where(match, hard_ref[pl.ds(step, 1), :], 0.0), axis=1, keepdims=True)
    table_ref[...] += jnp.where(iota(table_ref.shape, 1) == step, column, 0.0)


def weigh_slots(pos, hard, cap):
    n_data, rows = pos.shape
    return call(
        weigh_kernel,
        n_data,
        [whole((n_data, rows)), whole((n_data, rows))],
        whole((cap, n_data)),
        jax.ShapeDtypeStruct((cap, n_data), F32),
        4 * n_data * cap * rows,
        n_data * rows * 8,
    )(pos, hard)


def hard_grad_kernel(pos_ref, hard_ref, slot_ref, total_ref):
    step = pl.program_id(0)
    cap = slot_ref.shape[1]
    rows = pos_ref.shape[1]

    @pl.when(step == 0)
    def _():
        total_ref[...] = jnp.zeros_like(total_ref)

    match = iota((cap, rows), 0) == pos_ref[pl.ds(step, 1), :]
    spread = jnp.where(match, hard_ref[pl.ds(step, 1), :], 0.0).astype(BF16)
    total_ref[...] += contract(slot_ref[0], spread, 0, 0)


def hard_grad(pos, hard, p_slots):
    n_data, cap, piece = p_slots.shape
    rows = pos.shape[1]
    return call(
        hard_grad_kernel,
        n_data,
        [whole((n_data, rows)), whole((n_data, rows)), slab(cap, piece)],
        whole((piece, rows)),
        jax.ShapeDtypeStruct((piece, rows), F32),
        2 * n_data * cap * rows * piece,
        n_data * cap * piece * 2,
    )(pos, hard, p_slots)


def pair_kernel(scale, rows_ref, table_ref, q_ref, base_ref, total_ref):
    step = pl.program_id(0)
    cap = q_ref.shape[1]
    rows = total_ref.shape[0]

    @pl.when(step == 0)
    def _():
        total_ref[...] = base_ref[...] * scale

    weight = jnp.sum(
        jnp.where(iota(table_ref.shape, 1) == step, table_ref[...], 0.0), axis=1, keepdims=True
    )
    pairs = ((weight * scale) * q_ref[0].astype(F32)).astype(BF16)
    wanted = rows_ref[pl.ds(step, 1), :].astype(jnp.int32)
    match = jnp.where(iota((rows, cap), 0) == wanted, 1.0, 0.0).astype(BF16)
    total_ref[...] += contract(match, pairs, 1, 0)


def pair_grad(scale, wanted, table, q_received, base):
    n_data, cap, piece = q_received.shape
    rows = base.shape[0]
    return call(
        functools.partial(pair_kernel, scale),
        n_data,
        [whole((n_data, cap)), whole((cap, n_data)), slab(cap, piece), whole((rows, piece))],
        whole((rows, piece)),
        jax.ShapeDtypeStruct((rows, piece), F32),
        2 * n_data * cap * rows * piece,
        n_data * cap * piece * 2,
    )(wanted, table, q_received, base)


def swap(x, axis):
    return lax.all_to_all(x, axis, split_axis=0, concat_axis=0, tiled=True)


def group_total(x, n_members):
    return jnp.sum(lax.all_gather(x, "group", axis=0), axis=0)


def scatter_scores(scores, member, n_members):
    rows = scores.shape[0]
    share = rows // n_members
    half = n_members // 2
    split = scores.reshape(half, 2, share, rows)
    odd = (member % 2) == 1
    keep = jnp.where(odd, split[:, 1], split[:, 0])
    send = jnp.where(odd, split[:, 0], split[:, 1])
    pairs = [(i, i ^ 1) for i in range(n_members)]
    both = keep + lax.ppermute(send, "group", pairs)
    lanes = [[2 * y + core for y in range(half)] for core in range(2)]
    return lax.all_to_all(
        both, "group", split_axis=0, concat_axis=0, tiled=True, axis_index_groups=lanes
    )


def local(queries, passages, neg_owner, neg_row, gain):
    rows, piece = queries.shape
    negs = neg_owner.shape[1]
    n_data = lax.axis_size("dp")
    n_members = lax.axis_size("group")
    member = lax.axis_index("group")
    width = piece * n_members
    cap = min(rows, 5 * rows * negs // (4 * n_data))
    scale = 1.0 / (SOFTNESS_DIVISOR * math.sqrt(width))
    share = rows // n_members
    my_gain = lax.dynamic_slice_in_dim(gain, member * piece, piece, 0)

    p_all = lax.all_gather(passages, "dp", axis=0, tiled=True)

    q_values = queries.astype(F32)
    p_values = passages.astype(F32)
    squares = group_total(
        jnp.stack([jnp.sum(q_values * q_values, axis=1), jnp.sum(p_values * p_values, axis=1)]),
        n_members,
    )
    inverses = lax.rsqrt(squares / width + EPSILON)
    q_inverse, p_inverse = inverses[0][:, None], inverses[1][:, None]
    q_normed = q_values * q_inverse
    p_normed = p_values * p_inverse
    q_emb = (q_normed * my_gain).astype(BF16)
    p_emb = (p_normed * my_gain).astype(BF16)

    inverse_all = swap(jnp.broadcast_to(inverses[1][None, :], (n_data, rows)), "dp")
    pos, row_slots, column, q_slots = make_slots(neg_owner.T, neg_row.T, q_emb, n_data, cap)
    scores_part = contract(q_emb, p_emb, 1, 1) * scale
    scores = scatter_scores(scores_part, member, n_members)

    q_slots_late, p_all = lax.optimization_barrier((q_slots, p_all))
    q_received = swap(q_slots_late, "dp")

    p_slots, near_part = near_scores(
        scale, pos, column, inverse_all, my_gain[None, :], q_slots, p_all
    )
    near = swap(near_part.reshape(n_data, n_members, share).transpose(1, 0, 2), "group")
    near = jnp.maximum(jnp.sum(near, axis=0), ABSENT).T
    first = jnp.full((1,), member * share, jnp.int32)
    weights, hard, loss_part = softmax_share(first, scores, near)

    hard = lax.all_gather(hard, "group", axis=0, tiled=True).T.astype(F32)
    weights = lax.all_gather(weights, "group", axis=0, tiled=True)
    table = weigh_slots(pos, hard, cap)
    sent = jnp.stack([table.T, row_slots[:, 0, :]], axis=1)
    got = swap(sent, "dp")

    grad_q = (
        contract(weights, p_emb, 1, 0) + hard_grad(pos, hard, p_slots).T
    ) * scale
    batch_grad = contract(weights, q_emb, 0, 0)
    grad_p = pair_grad(scale, got[:, 1, :], got[:, 0, :].T, q_received, batch_grad)

    q_inner = grad_q * my_gain
    p_inner = grad_p * my_gain
    q_mean = group_total(jnp.sum(q_inner * q_normed, axis=1), n_members) / width
    p_mean = group_total(jnp.sum(p_inner * p_normed, axis=1), n_members) / width
    grad_queries = (q_inverse * (q_inner - q_normed * q_mean[:, None])).astype(BF16)
    grad_passages = (p_inverse * (p_inner - p_normed * p_mean[:, None])).astype(BF16)

    gain_part = jnp.sum(grad_q * q_normed, axis=0) + jnp.sum(grad_p * p_normed, axis=0)
    last = jnp.concatenate([gain_part, jnp.broadcast_to(loss_part[0], (128,))])
    last = jnp.sum(swap(jnp.broadcast_to(last[None, :], (n_data, piece + 128)), "dp"), axis=0)
    last = lax.all_gather(last, "group", axis=0)
    count = rows * n_data
    return (
        grad_queries,
        grad_passages,
        last[:, :piece].reshape(-1) / math.sqrt(count),
        jnp.sum(last[:, piece]) / count,
    )


def solution(mesh):
    return jax.shard_map(
        local,
        mesh=mesh,
        in_specs=(P("dp", "group"), P("dp", "group"), P("dp", None), P("dp", None), P()),
        out_specs=(P("dp", "group"), P("dp", "group"), P(), P()),
        check_vma=False,
    )
```

```python
import functools
import math

import jax
import jax.numpy as jnp
from jax import lax
from jax.experimental import pallas as pl
from jax.experimental.pallas import tpu as pltpu
from jax.sharding import PartitionSpec as P

EPSILON = 1e-06
SOFTNESS_DIVISOR = 0.25
F32 = jnp.float32
BF16 = jnp.bfloat16
VMEM_LIMIT = 52 * 1024 * 1024
MANY = 4


def iota(shape, axis):
    return lax.broadcasted_iota(jnp.int32, shape, axis)


def contract(a, b, da, db):
    return lax.dot_general(a, b, (((da,), (db,)), ((), ())), preferred_element_type=F32)


def cost(micros):
    return pl.CostEstimate(flops=0, bytes_accessed=int(micros * 3.5e6), transcendentals=0)


def call(kernel, grid, in_specs, out_specs, out_shape, micros, scratch=()):
    return pl.pallas_call(
        kernel,
        grid=(grid,),
        in_specs=in_specs,
        out_specs=out_specs,
        out_shape=out_shape,
        scratch_shapes=list(scratch),
        compiler_params=pltpu.CompilerParams(vmem_limit_bytes=VMEM_LIMIT),
        cost_estimate=cost(micros),
    )


def whole(shape):
    return pl.BlockSpec(shape, lambda i: (0,) * len(shape))


def slab(cap, piece, many=1):
    return pl.BlockSpec((many, cap, piece), lambda i: (i, 0, 0))


def table_column(table_ref, index):
    lanes = iota(table_ref.shape, 1)
    return jnp.sum(jnp.where(lanes == index, table_ref[...], 0.0), axis=1, keepdims=True)


def add_column(table_ref, index, column):
    table_ref[...] += jnp.where(iota(table_ref.shape, 1) == index, column, 0.0)


def slot_value(pos, values, cap):
    match = iota((cap, pos.shape[1]), 0) == pos
    return jnp.sum(jnp.where(match, values, 0.0), axis=1, keepdims=True)


def slot_pick(pos, values, cap):
    slots = iota((cap, pos.shape[1]), 0).astype(F32).astype(BF16)
    return jnp.where(slots == pos.astype(F32).astype(BF16), values, jnp.zeros((), BF16))


def one_hot(match):
    return jnp.where(match, 1.0, 0.0).astype(BF16)


def tables_kernel(owner_ref, row_ref, pos_ref, code_ref):
    negs, rows = owner_ref.shape
    n_data = pos_ref.shape[0]
    ids = iota((n_data, rows), 0)
    asked = jnp.full((n_data, rows), -1, jnp.int32)
    for k in range(negs):
        asked = jnp.where(owner_ref[k : k + 1, :] == ids, row_ref[k : k + 1, :], asked)
    hit = one_hot(asked >= 0)
    before = one_hot(iota((rows, rows), 0) < iota((rows, rows), 1))
    count = contract(hit, before, 1, 0).astype(jnp.int32)
    pos_ref[...] = jnp.where(asked >= 0, count, -1)
    code_ref[...] = jnp.where(asked >= 0, asked * 1024 + count, -1).astype(F32)


def make_tables(owner_t, row_t, n_data):
    negs, rows = owner_t.shape
    return call(
        tables_kernel,
        1,
        [whole((negs, rows)), whole((negs, rows))],
        [whole((n_data, rows)), whole((n_data, rows))],
        [
            jax.ShapeDtypeStruct((n_data, rows), jnp.int32),
            jax.ShapeDtypeStruct((n_data, rows), F32),
        ],
        1,
    )(owner_t, row_t)


def decode(code_ref, index):
    code = code_ref[pl.ds(index, 1), :].astype(jnp.int32)
    return code & 1023, code >> 10


def serve_kernel(code_ref, p_ref, slot_ref, pick_ref):
    many, cap, piece = slot_ref.shape
    rows = p_ref.shape[0]
    for t in range(many):
        pos, asked = decode(code_ref, pl.program_id(0) * many + t)
        wanted = slot_value(pos, (asked + 1).astype(F32), cap).astype(jnp.int32) - 1
        pick_ref[t * cap : (t + 1) * cap, :] = one_hot(iota((cap, rows), 1) == wanted)
    found = contract(pick_ref[...], p_ref[...], 1, 0).astype(BF16)
    slot_ref[...] = found.reshape(many, cap, piece)


def serve(code, passages, cap):
    n_data, rows = code.shape
    piece = passages.shape[1]
    return call(
        serve_kernel,
        n_data // MANY,
        [whole((n_data, rows)), whole((rows, piece))],
        slab(cap, piece, MANY),
        jax.ShapeDtypeStruct((n_data, cap, piece), BF16),
        8,
        [pltpu.VMEM((MANY * cap, rows), BF16)],
    )(code, passages)


def match_kernel(code_ref, match_ref):
    step = pl.program_id(0)
    rows, wide = match_ref.shape[1:]
    many = 4
    each = wide // many
    part = iota((8, rows), 0)
    for t in range(many):
        pos, asked = decode(code_ref, step * many + t)
        asked = asked + 1
        digits = jnp.where(part == 0, asked >> 5, jnp.where(part == 1, asked & 31, 0))
        pick = one_hot(iota((each, rows), 0) == pos)
        found = contract(digits.astype(F32).astype(BF16), pick, 1, 1)
        wanted = (found[0:1, :] * 32.0 + found[1:2, :]).astype(jnp.int32) - 1
        match_ref[0, :, t * each : (t + 1) * each] = one_hot(iota((rows, each), 0) == wanted)


def make_match(code, many, each):
    n_data, rows = code.shape
    wide = many * each
    steps = n_data // many
    return call(
        match_kernel,
        steps,
        [whole((n_data, rows))],
        slab(rows, wide),
        jax.ShapeDtypeStruct((steps, rows, wide), BF16),
        10,
    )(code)


def slots_kernel(pos_ref, q_ref, inverse_ref, slot_ref, table_ref, pick_ref):
    step = pl.program_id(0)
    many, cap, piece = slot_ref.shape

    @pl.when(step == 0)
    def _():
        table_ref[...] = jnp.zeros_like(table_ref)

    for t in range(many):
        pos = pos_ref[pl.ds(step * many + t, 1), :]
        pick_ref[t * cap : (t + 1) * cap, :] = slot_pick(pos, jnp.ones((), BF16), cap)
        add_column(table_ref, step * many + t, slot_value(pos, inverse_ref[...], cap))
    found = contract(pick_ref[...], q_ref[...], 1, 0).astype(BF16)
    slot_ref[...] = found.reshape(many, cap, piece)


def make_slots(pos, q_emb, inverse, cap):
    n_data, rows = pos.shape
    piece = q_emb.shape[1]
    return call(
        slots_kernel,
        n_data // MANY,
        [whole((n_data, rows)), whole((rows, piece)), whole((1, rows))],
        [slab(cap, piece, MANY), whole((cap, n_data))],
        [
            jax.ShapeDtypeStruct((n_data, cap, piece), BF16),
            jax.ShapeDtypeStruct((cap, n_data), F32),
        ],
        9,
        [pltpu.VMEM((MANY * cap, rows), BF16)],
    )(pos, q_emb, inverse)


def collect_kernel(base_ref, code_ref, q_ref, slot_ref):
    many, cap, _ = slot_ref.shape
    rows = code_ref.shape[1]
    for t in range(many):
        pos, _ = decode(code_ref, base_ref[0] + pl.program_id(0) * many + t)
        pick = slot_pick(pos, jnp.ones((), BF16), cap)
        found = contract(pick, q_ref[t * rows : (t + 1) * rows, :], 1, 0)
        slot_ref[t] = found.astype(BF16)


def collect(base, code, part, cap):
    n_data, rows = code.shape
    piece = part.shape[1]
    count = part.shape[0] // rows
    many = 2
    return call(
        collect_kernel,
        count // many,
        [
            pl.BlockSpec(memory_space=pltpu.SMEM),
            whole((n_data, rows)),
            pl.BlockSpec((many * rows, piece), lambda i: (i, 0)),
        ],
        slab(cap, piece, many),
        jax.ShapeDtypeStruct((count, cap, piece), BF16),
        0.5 * count,
    )(base, code, part)


def near_kernel(scale, pos_ref, owner_ref, q_ref, p_ref, near_ref):
    step = pl.program_id(0)
    many, cap, _ = q_ref.shape
    rows = pos_ref.shape[1]
    chunk = 48

    @pl.when(step == 0)
    def _():
        near_ref[...] = jnp.zeros_like(near_ref)

    for t in range(many):
        owner = step * many + t
        pos = pos_ref[pl.ds(owner, 1), :]
        spread = jnp.zeros((8, rows), F32)
        for start in range(0, cap, chunk):
            span = slice(start, start + chunk)
            product = q_ref[t, span, :].astype(F32) * p_ref[t, span, :].astype(F32)
            score = jnp.sum(product, axis=1, keepdims=True) * scale
            match = iota((chunk, rows), 0) + start == pos
            spread += jnp.sum(jnp.where(match, score, 0.0).reshape(chunk // 8, 8, rows), axis=0)
        spread = jnp.sum(spread, axis=0, keepdims=True)
        near_ref[...] += jnp.where(owner_ref[...] == owner, spread, 0.0)


def near_scores(scale, pos, owner_t, q_slots, p_slots):
    n_data, cap, piece = q_slots.shape
    negs, rows = owner_t.shape
    return call(
        functools.partial(near_kernel, scale),
        n_data // MANY,
        [whole((n_data, rows)), whole((negs, rows)), slab(cap, piece, MANY), slab(cap, piece, MANY)],
        whole((negs, rows)),
        jax.ShapeDtypeStruct((negs, rows), F32),
        9,
    )(pos, owner_t, q_slots, p_slots)


def batch_kernel(scores_ref, stats_ref):
    scores = scores_ref[...]
    top = jnp.max(scores, axis=1, keepdims=True)
    total = jnp.sum(jnp.exp(scores - top), axis=1, keepdims=True)
    stats_ref[...] = jnp.where(iota(stats_ref.shape, 1) == 0, top, total)


def batch_stats(scores):
    share, rows = scores.shape
    return call(
        batch_kernel,
        1,
        [whole((share, rows))],
        whole((share, 2)),
        jax.ShapeDtypeStruct((share, 2), F32),
        1,
    )(scores)


def softmax_kernel(owner_ref, near_ref, stats_ref, hard_ref, lse_ref):
    near = jnp.sum(near_ref[...], axis=0)
    batch_top = stats_ref[0:1, :]
    top = jnp.maximum(batch_top, jnp.max(near, axis=0, keepdims=True))
    total = stats_ref[1:2, :] * jnp.exp(batch_top - top) + jnp.sum(
        jnp.exp(near - top), axis=0, keepdims=True
    )
    lse = top + jnp.log(total)
    lse_ref[...] = lse
    hard = jnp.exp(near - lse).astype(BF16).astype(F32)
    ids = iota(hard_ref.shape, 0)
    spread = jnp.zeros(hard_ref.shape, F32)
    for k in range(hard.shape[0]):
        spread += jnp.where(owner_ref[k : k + 1, :] == ids, hard[k : k + 1, :], 0.0)
    hard_ref[...] = spread


def softmax_all(owner_t, near, stats, n_data):
    n_members, negs, rows = near.shape
    return call(
        softmax_kernel,
        1,
        [whole((negs, rows)), whole((n_members, negs, rows)), whole((2, rows))],
        [whole((n_data, rows)), whole((1, rows))],
        [jax.ShapeDtypeStruct((n_data, rows), F32), jax.ShapeDtypeStruct((1, rows), F32)],
        2,
    )(owner_t, near, stats)


def weigh_kernel(pos_ref, hard_ref, table_ref):
    step = pl.program_id(0)
    many = 8

    @pl.when(step == 0)
    def _():
        table_ref[...] = jnp.zeros_like(table_ref)

    lanes = iota(table_ref.shape, 1)
    total = table_ref[...]
    for t in range(many):
        at = step * many + t
        weight = slot_value(pos_ref[pl.ds(at, 1), :], hard_ref[pl.ds(at, 1), :], total.shape[0])
        total = jnp.where(lanes == at, weight, total)
    table_ref[...] = total


def weigh_slots(pos, hard, cap):
    n_data, rows = pos.shape
    return call(
        weigh_kernel,
        n_data // 8,
        [whole((n_data, rows)), whole((n_data, rows))],
        whole((cap, n_data)),
        jax.ShapeDtypeStruct((cap, n_data), F32),
        5,
    )(pos, hard)


def hard_grad_kernel(scale, pos_ref, hard_ref, table_ref, q_ref, p_ref, total_ref, sum_ref, spread_ref):
    step = pl.program_id(0)
    many, cap, piece = p_ref.shape

    @pl.when(step == 0)
    def _():
        total_ref[...] = jnp.zeros_like(total_ref)
        sum_ref[...] = jnp.zeros_like(sum_ref)

    gain = jnp.zeros((8, piece), F32)
    for t in range(many):
        at = step * many + t
        hard = hard_ref[pl.ds(at, 1), :].astype(BF16)
        spread_ref[t * cap : (t + 1) * cap, :] = slot_pick(pos_ref[pl.ds(at, 1), :], hard, cap)
        weight = table_column(table_ref, at) * scale
        pairs = (weight * q_ref[t].astype(F32)).astype(BF16).astype(F32)
        gain += jnp.sum((pairs * p_ref[t].astype(F32)).reshape(cap // 8, 8, piece), axis=0)
    sum_ref[...] += jnp.sum(gain, axis=0, keepdims=True)
    total_ref[...] += contract(p_ref[...].reshape(many * cap, piece), spread_ref[...], 0, 0)


def hard_grad(scale, pos, hard, table, q_slots, p_slots):
    n_data, cap, piece = p_slots.shape
    rows = pos.shape[1]
    return call(
        functools.partial(hard_grad_kernel, scale),
        n_data // MANY,
        [
            whole((n_data, rows)),
            whole((n_data, rows)),
            whole((cap, n_data)),
            slab(cap, piece, MANY),
            slab(cap, piece, MANY),
        ],
        [whole((piece, rows)), whole((1, piece))],
        [jax.ShapeDtypeStruct((piece, rows), F32), jax.ShapeDtypeStruct((1, piece), F32)],
        12,
        [pltpu.VMEM((MANY * cap, rows), BF16)],
    )(pos, hard, table, q_slots, p_slots)


def pair_kernel(scale, nz, x_ref, table_ref, inverse_ref, gain_ref, match_ref, *refs):
    q_refs, (total_ref, pairs_ref) = refs[:7], refs[7:]
    step = pl.program_id(0)
    many, cap, _ = q_refs[0].shape
    each = pairs_ref.shape[0] // many
    nx = pl.num_programs(0) * many // nz
    first = lax.rem(x_ref[0] * nz + step * many, nx * nz)

    @pl.when(step == 0)
    def _():
        total_ref[...] = jnp.zeros_like(total_ref)
        pairs_ref[...] = jnp.zeros_like(pairs_ref)

    def fill(q_ref):
        for t in range(many):
            weight = table_column(table_ref, first + t)
            inverse = table_column(inverse_ref, first + t)
            emb = ((q_ref[t].astype(F32) * inverse) * gain_ref[...]).astype(BF16)
            pairs = ((weight * scale) * emb.astype(F32)).astype(BF16)
            pairs_ref[t * each : t * each + cap, :] = pairs

    half = nz // many
    for place, (low, high) in enumerate(pair_spans(half)):
        pl.when((step >= low) & (step < high))(functools.partial(fill, q_refs[place]))
    total_ref[...] += contract(match_ref[0], pairs_ref[...], 1, 0)


def pair_spans(half):
    quarter = half // 2
    return [(0, half)] + [(half + i * quarter, half + (i + 1) * quarter) for i in range(6)]


def pair_grad(scale, nz, x, table, inverse, gain, match, parts):
    cap, n_data = table.shape
    steps, rows, wide = match.shape
    piece = parts[0].shape[2]
    many = n_data // steps

    def part_spec(span):
        low, high = span
        return pl.BlockSpec(
            (many, cap, piece), lambda i, x_ref: (jnp.clip(i, low, high - 1) - low, 0, 0)
        )

    def match_block(i, x_ref):
        return (lax.rem(x_ref[0] * (nz // many) + i, steps), 0, 0)

    return pl.pallas_call(
        functools.partial(pair_kernel, scale, nz),
        grid_spec=pltpu.PrefetchScalarGridSpec(
            num_scalar_prefetch=1,
            grid=(steps,),
            in_specs=[
                pl.BlockSpec((cap, n_data), lambda i, x_ref: (0, 0)),
                pl.BlockSpec((cap, n_data), lambda i, x_ref: (0, 0)),
                pl.BlockSpec((1, piece), lambda i, x_ref: (0, 0)),
                pl.BlockSpec((1, rows, wide), match_block),
                *[part_spec(span) for span in pair_spans(nz // many)],
            ],
            out_specs=pl.BlockSpec((rows, piece), lambda i, x_ref: (0, 0)),
            scratch_shapes=[pltpu.VMEM((wide, piece), BF16)],
        ),
        out_shape=jax.ShapeDtypeStruct((rows, piece), F32),
        compiler_params=pltpu.CompilerParams(vmem_limit_bytes=VMEM_LIMIT),
        cost_estimate=cost(7),
    )(x, table, inverse, gain, match, *parts)


def swap(x, axis):
    return lax.all_to_all(x, axis, split_axis=0, concat_axis=0, tiled=True)


def tied(*values):
    return lax.optimization_barrier(values)


class Torus:
    def __init__(self, n_data, nx):
        self.nx, self.nz = nx, n_data // nx
        self.along_z = [[x * self.nz + z for z in range(self.nz)] for x in range(nx)]

    def shift(self, value, by):
        nx, nz = self.nx, self.nz
        pairs = [
            (x * nz + z, (x + by) % nx * nz + z) for x in range(nx) for z in range(nz)
        ]
        return lax.ppermute(value, "dp", pairs)

    def gather_z(self, value):
        return lax.all_gather(value, "dp", axis=0, tiled=True, axis_index_groups=self.along_z)


def local(nx, queries, passages, neg_owner, neg_row, gain):
    rows, piece = queries.shape
    negs = neg_owner.shape[1]
    n_data = lax.axis_size("dp")
    n_members = lax.axis_size("group")
    member = lax.axis_index("group")
    width = piece * n_members
    cap = min(rows, 5 * rows * negs // (4 * n_data))
    scale = 1.0 / (SOFTNESS_DIVISOR * math.sqrt(width))
    torus = Torus(n_data, nx)
    nz = torus.nz
    my_x = (lax.axis_index("dp") // nz).astype(jnp.int32)
    my_gain = lax.dynamic_slice_in_dim(gain, member * piece, piece, 0)
    gain_row = my_gain[None, :]
    owner_t = neg_owner.T

    def base(away, more=0):
        return jnp.full((1,), (my_x + away) % nx * nz + more, jnp.int32)

    q_zero = torus.gather_z(queries)
    half = q_zero.shape[0] // 2

    pos, code = make_tables(owner_t, neg_row.T, n_data)
    code_got = swap(code, "dp")

    q_values = queries.astype(F32)
    p_values = passages.astype(F32)
    squares = jnp.stack(
        [jnp.sum(q_values * q_values, axis=1), jnp.sum(p_values * p_values, axis=1)]
    )
    squares = jnp.sum(lax.all_gather(squares, "group", axis=0), axis=0)
    squares, code_got = tied(squares, code_got)
    inverses = lax.rsqrt(squares / width + EPSILON)
    q_inverse, p_inverse = inverses[0][:, None], inverses[1][:, None]
    q_normed = q_values * q_inverse
    p_normed = p_values * p_inverse
    q_emb = (q_normed * my_gain).astype(BF16)
    p_emb = (p_normed * my_gain).astype(BF16)
    p_slots = swap(serve(code_got, p_emb, cap), "dp")

    scores = contract(q_emb, p_emb, 1, 1) * scale
    scores = lax.psum_scatter(scores, "group", scatter_dimension=0, tiled=True)
    q_slots, inverse = make_slots(pos, q_emb, inverses[:1], cap)
    each = -(-cap // 128) * 128
    match = make_match(code_got, 4, each)
    q_three_low, q_one_high = torus.shift(q_zero[:half], 1), torus.shift(q_zero[half:], -1)
    part_zero = collect(base(0), code_got, q_zero, cap)
    scores, q_slots, match, q_three_low, q_one_high, q_zero, part_zero = tied(
        scores, q_slots, match, q_three_low, q_one_high, q_zero, part_zero
    )
    stats = batch_stats(scores)
    scores = lax.all_gather(scores, "group", axis=0, tiled=True)
    q_one_low, q_three_high = torus.shift(q_zero[:half], -1), torus.shift(q_zero[half:], 1)
    q_low, q_high = torus.shift(q_three_low, 1), torus.shift(q_one_high, -1)
    p_slots, stats = tied(p_slots, stats)

    near = near_scores(scale, pos, owner_t, q_slots, p_slots)
    share = rows // n_members
    per = 2 * share // negs
    stats = jnp.pad(stats.T.reshape(negs, per), ((0, 0), (0, -per % 128)))
    mixed = lax.all_gather(jnp.concatenate([near, stats], axis=1), "group", axis=0)
    near = mixed[:, :, :rows]
    stats = mixed[:, :, rows : rows + per].reshape(n_members, 2, share)
    stats = stats.transpose(1, 0, 2).reshape(2, rows)
    hard, lse = softmax_all(owner_t, near, stats, n_data)
    table = weigh_slots(pos, hard, cap)
    _, q_one_low, q_one_high, q_low, q_high, q_three_low, q_three_high = tied(
        hard, q_one_low, q_one_high, q_low, q_high, q_three_low, q_three_high
    )
    got = swap(jnp.concatenate([table, inverse], axis=0).T, "dp").T

    parts = [part_zero] + [
        collect(at, code_got, part, cap)
        for at, part in (
            (base(1), q_one_low),
            (base(1, nz // 2), q_one_high),
            (base(2), q_low),
            (base(2, nz // 2), q_high),
            (base(3), q_three_low),
            (base(3, nz // 2), q_three_high),
        )
    ]

    hard_q, pair_gain = hard_grad(scale, pos, hard, table, q_slots, p_slots)
    lse = lse[0][:, None]
    positive = iota((rows, rows), 0) == iota((rows, rows), 1)
    weights = (jnp.exp(scores - lse) - positive.astype(F32)).astype(BF16)
    losses = jnp.sum(lse) - jnp.sum(jnp.where(positive, scores, 0.0))
    grad_q = (contract(weights, p_emb, 1, 0) + hard_q.T) * scale
    batch_grad = contract(weights, q_emb, 0, 0) * scale
    gain_part = (
        jnp.sum(grad_q * q_normed, axis=0)
        + jnp.sum(batch_grad * p_normed, axis=0)
        + pair_gain[0] / my_gain
    )
    last = jnp.concatenate([gain_part, jnp.broadcast_to(losses, (128,))])
    last, got = tied(last, got)
    last = jnp.sum(swap(jnp.broadcast_to(last[None, :], (n_data, piece + 128)), "dp"), axis=0)

    grad_p = batch_grad + pair_grad(
        scale, nz, jnp.full((1,), my_x), got[:cap], got[cap:], gain_row, match, parts
    )
    q_inner = grad_q * my_gain
    p_inner = grad_p * my_gain
    final = jnp.concatenate(
        [jnp.sum(q_inner * q_normed, axis=1), jnp.sum(p_inner * p_normed, axis=1), last]
    )
    final = lax.all_gather(final, "group", axis=0)
    means = jnp.sum(final[:, : 2 * rows], axis=0) / width
    q_mean, p_mean = means[:rows, None], means[rows:, None]
    grad_queries = (q_inverse * (q_inner - q_normed * q_mean)).astype(BF16)
    grad_passages = (p_inverse * (p_inner - p_normed * p_mean)).astype(BF16)
    count = rows * n_data
    grad_gain = final[:, 2 * rows : 2 * rows + piece].reshape(-1) / math.sqrt(count)
    loss = final[0, 2 * rows + piece] / count
    return grad_queries, grad_passages, grad_gain, loss


def solution(mesh):
    nx = 4
    return jax.shard_map(
        functools.partial(local, nx),
        mesh=mesh,
        in_specs=(P("dp", "group"), P("dp", "group"), P("dp", None), P("dp", None), P()),
        out_specs=(P("dp", "group"), P("dp", "group"), P(), P()),
        check_vma=False,
    )
```

```python
import functools
import math

import jax
import jax.numpy as jnp
from jax import lax
from jax.experimental import pallas as pl
from jax.experimental.pallas import tpu as pltpu
from jax.sharding import PartitionSpec as P

EPSILON = 1e-06
SOFTNESS_DIVISOR = 0.25
F32 = jnp.float32
BF16 = jnp.bfloat16
VMEM_LIMIT = 52 * 1024 * 1024
MANY = 4


def iota(shape, axis):
    return lax.broadcasted_iota(jnp.int32, shape, axis)


def contract(a, b, da, db):
    return lax.dot_general(a, b, (((da,), (db,)), ((), ())), preferred_element_type=F32)


def cost(micros):
    return pl.CostEstimate(flops=0, bytes_accessed=int(micros * 3.5e6), transcendentals=0)


def call(kernel, grid, in_specs, out_specs, out_shape, micros, scratch=()):
    return pl.pallas_call(
        kernel,
        grid=(grid,),
        in_specs=in_specs,
        out_specs=out_specs,
        out_shape=out_shape,
        scratch_shapes=list(scratch),
        compiler_params=pltpu.CompilerParams(vmem_limit_bytes=VMEM_LIMIT),
        cost_estimate=cost(micros),
    )


def whole(shape):
    return pl.BlockSpec(shape, lambda i: (0,) * len(shape))


def slab(cap, piece, many=1):
    return pl.BlockSpec((many, cap, piece), lambda i: (i, 0, 0))


def table_column(table_ref, index):
    lanes = iota(table_ref.shape, 1)
    return jnp.sum(jnp.where(lanes == index, table_ref[...], 0.0), axis=1, keepdims=True)


def add_column(table_ref, index, column):
    table_ref[...] += jnp.where(iota(table_ref.shape, 1) == index, column, 0.0)


def slot_value(pos, values, cap):
    match = iota((cap, pos.shape[1]), 0) == pos
    return jnp.sum(jnp.where(match, values, 0.0), axis=1, keepdims=True)


def slot_pick(pos, values, cap):
    slots = iota((cap, pos.shape[1]), 0).astype(F32).astype(BF16)
    return jnp.where(slots == pos.astype(F32).astype(BF16), values, jnp.zeros((), BF16))


def one_hot(match):
    return jnp.where(match, 1.0, 0.0).astype(BF16)


def tables_kernel(owner_ref, row_ref, pos_ref, code_ref):
    negs, rows = owner_ref.shape
    n_data = pos_ref.shape[0]
    ids = iota((n_data, rows), 0)
    asked = jnp.full((n_data, rows), -1, jnp.int32)
    for k in range(negs):
        asked = jnp.where(owner_ref[k : k + 1, :] == ids, row_ref[k : k + 1, :], asked)
    hit = one_hot(asked >= 0)
    before = one_hot(iota((rows, rows), 0) < iota((rows, rows), 1))
    count = contract(hit, before, 1, 0).astype(jnp.int32)
    pos_ref[...] = jnp.where(asked >= 0, count, -1)
    code_ref[...] = jnp.where(asked >= 0, asked * 1024 + count, -1).astype(F32)


def make_tables(owner_t, row_t, n_data):
    negs, rows = owner_t.shape
    return call(
        tables_kernel,
        1,
        [whole((negs, rows)), whole((negs, rows))],
        [whole((n_data, rows)), whole((n_data, rows))],
        [
            jax.ShapeDtypeStruct((n_data, rows), jnp.int32),
            jax.ShapeDtypeStruct((n_data, rows), F32),
        ],
        1,
    )(owner_t, row_t)


def decode(code_ref, index):
    code = code_ref[pl.ds(index, 1), :].astype(jnp.int32)
    return code & 1023, code >> 10


def serve_kernel(code_ref, p_ref, slot_ref, pick_ref):
    many, cap, piece = slot_ref.shape
    rows = p_ref.shape[0]
    for t in range(many):
        pos, asked = decode(code_ref, pl.program_id(0) * many + t)
        wanted = slot_value(pos, (asked + 1).astype(F32), cap).astype(jnp.int32) - 1
        pick_ref[t * cap : (t + 1) * cap, :] = one_hot(iota((cap, rows), 1) == wanted)
    found = contract(pick_ref[...], p_ref[...], 1, 0).astype(BF16)
    slot_ref[...] = found.reshape(many, cap, piece)


def serve(code, passages, cap):
    n_data, rows = code.shape
    piece = passages.shape[1]
    return call(
        serve_kernel,
        n_data // MANY,
        [whole((n_data, rows)), whole((rows, piece))],
        slab(cap, piece, MANY),
        jax.ShapeDtypeStruct((n_data, cap, piece), BF16),
        8,
        [pltpu.VMEM((MANY * cap, rows), BF16)],
    )(code, passages)


def match_kernel(code_ref, match_ref):
    rows = match_ref.shape[2]
    cap = match_ref.shape[1] // MANY
    for t in range(MANY):
        pos, asked = decode(code_ref, pl.program_id(0) * MANY + t)
        wanted = slot_value(pos, (asked + 1).astype(F32), cap).astype(jnp.int32) - 1
        match_ref[0, t * cap : (t + 1) * cap, :] = one_hot(iota((cap, rows), 1) == wanted)


def make_match(code, cap):
    n_data, rows = code.shape
    steps = n_data // MANY
    return call(
        match_kernel,
        steps,
        [whole((n_data, rows))],
        slab(MANY * cap, rows),
        jax.ShapeDtypeStruct((steps, MANY * cap, rows), BF16),
        8,
    )(code)


def slots_kernel(pos_ref, q_ref, inverse_ref, slot_ref, table_ref, pick_ref):
    step = pl.program_id(0)
    many, cap, piece = slot_ref.shape

    @pl.when(step == 0)
    def _():
        table_ref[...] = jnp.zeros_like(table_ref)

    for t in range(many):
        pos = pos_ref[pl.ds(step * many + t, 1), :]
        pick_ref[t * cap : (t + 1) * cap, :] = slot_pick(pos, jnp.ones((), BF16), cap)
        add_column(table_ref, step * many + t, slot_value(pos, inverse_ref[...], cap))
    found = contract(pick_ref[...], q_ref[...], 1, 0).astype(BF16)
    slot_ref[...] = found.reshape(many, cap, piece)


def make_slots(pos, q_emb, inverse, cap):
    n_data, rows = pos.shape
    piece = q_emb.shape[1]
    return call(
        slots_kernel,
        n_data // MANY,
        [whole((n_data, rows)), whole((rows, piece)), whole((1, rows))],
        [slab(cap, piece, MANY), whole((cap, n_data))],
        [
            jax.ShapeDtypeStruct((n_data, cap, piece), BF16),
            jax.ShapeDtypeStruct((cap, n_data), F32),
        ],
        9,
        [pltpu.VMEM((MANY * cap, rows), BF16)],
    )(pos, q_emb, inverse)


def collect_kernel(first, counts, base_ref, code_ref, *refs):
    q_refs, slot_ref = refs[:-1], refs[-1]
    step = pl.program_id(0)
    many, cap, _ = slot_ref.shape
    rows = code_ref.shape[1]

    def fill(q_ref, source):
        for t in range(many):
            pos, _ = decode(code_ref, source + t)
            pick = slot_pick(pos, jnp.ones((), BF16), cap)
            found = contract(pick, q_ref[t * rows : (t + 1) * rows, :], 1, 0)
            slot_ref[t] = found.astype(BF16)

    start = 0
    for place, count in enumerate(counts):
        source = base_ref[first + place] + (step - start) * many
        pl.when((step >= start) & (step < start + count))(
            functools.partial(fill, q_refs[place], source)
        )
        start += count


def collect(base, first, code, cap, parts):
    n_data, rows = code.shape
    piece = parts[0].shape[1]
    many = 2
    counts = [part.shape[0] // (rows * many) for part in parts]
    starts = [sum(counts[:i]) for i in range(len(counts))]

    def spec(start, count):
        return pl.BlockSpec(
            (many * rows, piece), lambda i: (jnp.clip(i - start, 0, count - 1), 0)
        )

    steps = sum(counts)
    return call(
        functools.partial(collect_kernel, first, counts),
        steps,
        [
            pl.BlockSpec(memory_space=pltpu.SMEM),
            whole((n_data, rows)),
            *[spec(start, count) for start, count in zip(starts, counts)],
        ],
        slab(cap, piece, many),
        jax.ShapeDtypeStruct((steps * many, cap, piece), BF16),
        0.3 * steps * many,
    )(base, code, *parts)


def near_kernel(scale, pos_ref, owner_ref, q_ref, p_ref, near_ref):
    step = pl.program_id(0)
    many, cap, _ = q_ref.shape
    rows = pos_ref.shape[1]
    chunk = 48

    @pl.when(step == 0)
    def _():
        near_ref[...] = jnp.zeros_like(near_ref)

    for t in range(many):
        owner = step * many + t
        pos = pos_ref[pl.ds(owner, 1), :]
        spread = jnp.zeros((8, rows), F32)
        for start in range(0, cap, chunk):
            span = slice(start, start + chunk)
            product = q_ref[t, span, :].astype(F32) * p_ref[t, span, :].astype(F32)
            score = jnp.sum(product, axis=1, keepdims=True) * scale
            match = iota((chunk, rows), 0) + start == pos
            spread += jnp.sum(jnp.where(match, score, 0.0).reshape(chunk // 8, 8, rows), axis=0)
        spread = jnp.sum(spread, axis=0, keepdims=True)
        near_ref[...] += jnp.where(owner_ref[...] == owner, spread, 0.0)


def near_scores(scale, pos, owner_t, q_slots, p_slots):
    n_data, cap, piece = q_slots.shape
    negs, rows = owner_t.shape
    return call(
        functools.partial(near_kernel, scale),
        n_data // MANY,
        [whole((n_data, rows)), whole((negs, rows)), slab(cap, piece, MANY), slab(cap, piece, MANY)],
        whole((negs, rows)),
        jax.ShapeDtypeStruct((negs, rows), F32),
        9,
    )(pos, owner_t, q_slots, p_slots)


def batch_kernel(scores_ref, stats_ref):
    scores = scores_ref[...]
    top = jnp.max(scores, axis=1, keepdims=True)
    total = jnp.sum(jnp.exp(scores - top), axis=1, keepdims=True)
    stats_ref[...] = jnp.where(iota(stats_ref.shape, 1) == 0, top, total)


def batch_stats(scores):
    share, rows = scores.shape
    return call(
        batch_kernel,
        1,
        [whole((share, rows))],
        whole((share, 2)),
        jax.ShapeDtypeStruct((share, 2), F32),
        1,
    )(scores)


def softmax_kernel(owner_ref, near_ref, stats_ref, hard_ref, lse_ref):
    near = jnp.sum(near_ref[...], axis=0)
    batch_top = stats_ref[0:1, :]
    top = jnp.maximum(batch_top, jnp.max(near, axis=0, keepdims=True))
    total = stats_ref[1:2, :] * jnp.exp(batch_top - top) + jnp.sum(
        jnp.exp(near - top), axis=0, keepdims=True
    )
    lse = top + jnp.log(total)
    lse_ref[...] = lse
    hard = jnp.exp(near - lse).astype(BF16).astype(F32)
    ids = iota(hard_ref.shape, 0)
    spread = jnp.zeros(hard_ref.shape, F32)
    for k in range(hard.shape[0]):
        spread += jnp.where(owner_ref[k : k + 1, :] == ids, hard[k : k + 1, :], 0.0)
    hard_ref[...] = spread


def softmax_all(owner_t, near, stats, n_data):
    n_members, negs, rows = near.shape
    return call(
        softmax_kernel,
        1,
        [whole((negs, rows)), whole((n_members, negs, rows)), whole((2, rows))],
        [whole((n_data, rows)), whole((1, rows))],
        [jax.ShapeDtypeStruct((n_data, rows), F32), jax.ShapeDtypeStruct((1, rows), F32)],
        2,
    )(owner_t, near, stats)


def weigh_kernel(pos_ref, hard_ref, table_ref):
    step = pl.program_id(0)
    many = 8

    @pl.when(step == 0)
    def _():
        table_ref[...] = jnp.zeros_like(table_ref)

    lanes = iota(table_ref.shape, 1)
    total = table_ref[...]
    for t in range(many):
        at = step * many + t
        weight = slot_value(pos_ref[pl.ds(at, 1), :], hard_ref[pl.ds(at, 1), :], total.shape[0])
        total = jnp.where(lanes == at, weight, total)
    table_ref[...] = total


def weigh_slots(pos, hard, cap):
    n_data, rows = pos.shape
    return call(
        weigh_kernel,
        n_data // 8,
        [whole((n_data, rows)), whole((n_data, rows))],
        whole((cap, n_data)),
        jax.ShapeDtypeStruct((cap, n_data), F32),
        5,
    )(pos, hard)


def hard_grad_kernel(scale, pos_ref, hard_ref, table_ref, q_ref, p_ref, total_ref, sum_ref, spread_ref):
    step = pl.program_id(0)
    many, cap, piece = p_ref.shape

    @pl.when(step == 0)
    def _():
        total_ref[...] = jnp.zeros_like(total_ref)
        sum_ref[...] = jnp.zeros_like(sum_ref)

    gain = jnp.zeros((8, piece), F32)
    for t in range(many):
        at = step * many + t
        hard = hard_ref[pl.ds(at, 1), :].astype(BF16)
        spread_ref[t * cap : (t + 1) * cap, :] = slot_pick(pos_ref[pl.ds(at, 1), :], hard, cap)
        weight = table_column(table_ref, at) * scale
        pairs = (weight * q_ref[t].astype(F32)).astype(BF16).astype(F32)
        gain += jnp.sum((pairs * p_ref[t].astype(F32)).reshape(cap // 8, 8, piece), axis=0)
    sum_ref[...] += jnp.sum(gain, axis=0, keepdims=True)
    total_ref[...] += contract(p_ref[...].reshape(many * cap, piece), spread_ref[...], 0, 0)


def hard_grad(scale, pos, hard, table, q_slots, p_slots):
    n_data, cap, piece = p_slots.shape
    rows = pos.shape[1]
    return call(
        functools.partial(hard_grad_kernel, scale),
        n_data // MANY,
        [
            whole((n_data, rows)),
            whole((n_data, rows)),
            whole((cap, n_data)),
            slab(cap, piece, MANY),
            slab(cap, piece, MANY),
        ],
        [whole((piece, rows)), whole((1, piece))],
        [jax.ShapeDtypeStruct((piece, rows), F32), jax.ShapeDtypeStruct((1, piece), F32)],
        12,
        [pltpu.VMEM((MANY * cap, rows), BF16)],
    )(pos, hard, table, q_slots, p_slots)


def pair_kernel(scale, spans, base_ref, table_ref, gain_ref, match_ref, *refs):
    q_refs, (total_ref, pairs_ref, split_ref) = refs[: len(spans)], refs[len(spans) :]
    step = pl.program_id(0)
    many, cap, piece = q_refs[0].shape
    wide = table_ref.shape[1]
    n_data = wide // 4

    @pl.when(step == 0)
    def _():
        total_ref[...] = jnp.zeros_like(total_ref)
        table = table_ref[...]
        high = table.astype(BF16).astype(F32)
        middle = (table - high).astype(BF16).astype(F32)
        low = table - high - middle
        place = iota(table.shape, 1) // n_data
        split = jnp.where(place == 3, low, jnp.where(place == 2, middle, high))
        split_ref[...] = split.astype(BF16)

    lane = iota((wide, many * 128), 0)
    wanted = base_ref[step] + iota((wide, many * 128), 1) // 128
    weights = contract(split_ref[...], one_hot(lane == wanted), 1, 0) * scale
    spread = (lane >= n_data) & (lane % n_data == wanted)
    inverses = contract(split_ref[...], one_hot(spread), 1, 0)

    def fill(q_ref):
        for t in range(many):
            for lanes in range(0, piece, 128):
                span = slice(lanes, lanes + 128)
                raw = q_ref[t, :, span].astype(F32)
                column = slice(t * 128, (t + 1) * 128)
                emb = ((raw * inverses[:, column]) * gain_ref[:, span]).astype(BF16)
                pairs = (weights[:, column] * emb.astype(F32)).astype(BF16)
                pairs_ref[t * cap : (t + 1) * cap, span] = pairs

    for place, (low, high) in enumerate(spans):
        pl.when((step >= low) & (step < high))(functools.partial(fill, q_refs[place]))
    total_ref[...] += contract(pairs_ref[...], match_ref[0], 0, 0)


def pair_grad(scale, base, table, gain, match, parts):
    cap, wide = table.shape
    steps, deep, rows = match.shape
    piece = parts[0].shape[2]
    many = wide // 4 // steps
    ends = [sum(part.shape[0] for part in parts[: i + 1]) // many for i in range(len(parts))]
    spans = list(zip([0] + ends[:-1], ends))

    def part_spec(span):
        low, high = span
        return pl.BlockSpec(
            (many, cap, piece), lambda i, base_ref: (jnp.clip(i, low, high - 1) - low, 0, 0)
        )

    return pl.pallas_call(
        functools.partial(pair_kernel, scale, spans),
        grid_spec=pltpu.PrefetchScalarGridSpec(
            num_scalar_prefetch=1,
            grid=(steps,),
            in_specs=[
                pl.BlockSpec((cap, wide), lambda i, base_ref: (0, 0)),
                pl.BlockSpec((1, piece), lambda i, base_ref: (0, 0)),
                pl.BlockSpec((1, deep, rows), lambda i, base_ref: (base_ref[i] // many, 0, 0)),
                *[part_spec(span) for span in spans],
            ],
            out_specs=pl.BlockSpec((piece, rows), lambda i, base_ref: (0, 0)),
            scratch_shapes=[pltpu.VMEM((deep, piece), BF16), pltpu.VMEM((cap, wide), BF16)],
        ),
        out_shape=jax.ShapeDtypeStruct((piece, rows), F32),
        compiler_params=pltpu.CompilerParams(vmem_limit_bytes=VMEM_LIMIT),
        cost_estimate=cost(10),
    )(base, table, gain, match, *parts)


def swap(x, axis):
    return lax.all_to_all(x, axis, split_axis=0, concat_axis=0, tiled=True)


def tied(*values):
    return lax.optimization_barrier(values)


class Torus:
    def __init__(self, n_data, nx):
        self.nx, self.nz = nx, n_data // nx
        self.along_z = [[x * self.nz + z for z in range(self.nz)] for x in range(nx)]

    def shift(self, value, by):
        nx, nz = self.nx, self.nz
        pairs = [
            (x * nz + z, (x + by) % nx * nz + z) for x in range(nx) for z in range(nz)
        ]
        return lax.ppermute(value, "dp", pairs)

    def gather_z(self, value):
        return lax.all_gather(value, "dp", axis=0, tiled=True, axis_index_groups=self.along_z)


def local(nx, queries, passages, neg_owner, neg_row, gain):
    rows, piece = queries.shape
    negs = neg_owner.shape[1]
    n_data = lax.axis_size("dp")
    n_members = lax.axis_size("group")
    member = lax.axis_index("group")
    width = piece * n_members
    cap = min(rows, 5 * rows * negs // (4 * n_data))
    scale = 1.0 / (SOFTNESS_DIVISOR * math.sqrt(width))
    torus = Torus(n_data, nx)
    nz = torus.nz
    my_x = (lax.axis_index("dp") // nz).astype(jnp.int32)
    my_gain = lax.dynamic_slice_in_dim(gain, member * piece, piece, 0)
    gain_row = my_gain[None, :]
    owner_t = neg_owner.T

    away = jnp.array([0, 0, 3, 1, 1, 3, 2, 2], jnp.int32)
    upper = jnp.array([0, 1, 0, 1, 0, 1, 0, 1], jnp.int32)
    base = (my_x + away) % nx * nz + upper * (nz // 2)

    q_zero = torus.gather_z(queries)
    half = q_zero.shape[0] // 2

    pos, code = make_tables(owner_t, neg_row.T, n_data)
    code_got = swap(code, "dp")

    q_values = queries.astype(F32)
    p_values = passages.astype(F32)
    squares = jnp.stack(
        [jnp.sum(q_values * q_values, axis=1), jnp.sum(p_values * p_values, axis=1)]
    )
    squares = jnp.sum(lax.all_gather(squares, "group", axis=0), axis=0)
    squares, code_got = tied(squares, code_got)
    inverses = lax.rsqrt(squares / width + EPSILON)
    q_inverse, p_inverse = inverses[0][:, None], inverses[1][:, None]
    q_normed = q_values * q_inverse
    p_normed = p_values * p_inverse
    q_emb = (q_normed * my_gain).astype(BF16)
    p_emb = (p_normed * my_gain).astype(BF16)
    p_slots = swap(serve(code_got, p_emb, cap), "dp")

    scores = contract(q_emb, p_emb, 1, 1) * scale
    scores = lax.psum_scatter(scores, "group", scatter_dimension=0, tiled=True)
    q_slots, inverse = make_slots(pos, q_emb, inverses[:1], cap)
    match = make_match(code_got, cap)
    q_lower, q_upper = q_zero[:half], q_zero[half:]
    q_three_low, q_one_high = torus.shift(q_lower, 1), torus.shift(q_upper, -1)
    part_zero = collect(base, 0, code_got, cap, [q_zero])
    scores, q_slots, match, q_three_low, q_one_high, q_lower, q_upper, part_zero = tied(
        scores, q_slots, match, q_three_low, q_one_high, q_lower, q_upper, part_zero
    )
    stats = batch_stats(scores)
    scores = lax.all_gather(scores, "group", axis=0, tiled=True)
    q_one_low, q_three_high = torus.shift(q_lower, -1), torus.shift(q_upper, 1)
    q_low, q_high = torus.shift(q_three_low, 1), torus.shift(q_one_high, -1)
    part_first = collect(base, 2, code_got, cap, [q_three_low, q_one_high])
    p_slots, stats, part_first = tied(p_slots, stats, part_first)

    near = near_scores(scale, pos, owner_t, q_slots, p_slots)
    share = rows // n_members
    per = 2 * share // negs
    stats = jnp.pad(stats.T.reshape(negs, per), ((0, 0), (0, -per % 128)))
    mixed = lax.all_gather(jnp.concatenate([near, stats], axis=1), "group", axis=0)
    near = mixed[:, :, :rows]
    stats = mixed[:, :, rows : rows + per].reshape(n_members, 2, share)
    stats = stats.transpose(1, 0, 2).reshape(2, rows)
    hard, lse = softmax_all(owner_t, near, stats, n_data)
    table = weigh_slots(pos, hard, cap)
    hard_q, pair_gain = hard_grad(scale, pos, hard, table, q_slots, p_slots)
    lse = lse[0][:, None]
    positive = iota((rows, rows), 0) == iota((rows, rows), 1)
    weights = (jnp.exp(scores - lse) - positive.astype(F32)).astype(BF16)
    losses = jnp.sum(lse) - jnp.sum(jnp.where(positive, scores, 0.0))
    grad_q = (contract(weights, p_emb, 1, 0) + hard_q.T) * scale
    batch_grad = contract(weights, q_emb, 0, 0) * scale
    gain_part = (
        jnp.sum(grad_q * q_normed, axis=0)
        + jnp.sum(batch_grad * p_normed, axis=0)
        + pair_gain[0] / my_gain
    )
    last = jnp.concatenate([gain_part, jnp.broadcast_to(losses, (128,))])
    _, q_one_low, q_three_high, q_low, q_high = tied(last, q_one_low, q_three_high, q_low, q_high)
    sent = jnp.concatenate([table, inverse, jnp.zeros((-2 * cap % 128, n_data), F32)], axis=0).T
    edge = sent.shape[1]
    sent = jnp.concatenate([sent, jnp.broadcast_to(last[None, :], (n_data, piece + 128))], axis=1)
    got = swap(sent, "dp")
    last = jnp.sum(got[:, edge:], axis=0)
    got_weights, got_inverses = got[:, :cap].T, got[:, cap : 2 * cap].T
    table = jnp.concatenate([got_weights] + [got_inverses] * 3, axis=1)

    part_last = collect(base, 4, code_got, cap, [q_one_low, q_three_high, q_low, q_high])
    parts = [part_zero, part_first, part_last]
    grad_p = batch_grad + pair_grad(scale, base, table, gain_row, match, parts).T
    q_inner = grad_q * my_gain
    p_inner = grad_p * my_gain
    final = jnp.concatenate(
        [jnp.sum(q_inner * q_normed, axis=1), jnp.sum(p_inner * p_normed, axis=1), last]
    )
    final = lax.all_gather(final, "group", axis=0)
    means = jnp.sum(final[:, : 2 * rows], axis=0) / width
    q_mean, p_mean = means[:rows, None], means[rows:, None]
    grad_queries = (q_inverse * (q_inner - q_normed * q_mean)).astype(BF16)
    grad_passages = (p_inverse * (p_inner - p_normed * p_mean)).astype(BF16)
    count = rows * n_data
    grad_gain = final[:, 2 * rows : 2 * rows + piece].reshape(-1) / math.sqrt(count)
    loss = final[0, 2 * rows + piece] / count
    return grad_queries, grad_passages, grad_gain, loss


def solution(mesh):
    nx = 4
    return jax.shard_map(
        functools.partial(local, nx),
        mesh=mesh,
        in_specs=(P("dp", "group"), P("dp", "group"), P("dp", None), P("dp", None), P()),
        out_specs=(P("dp", "group"), P("dp", "group"), P(), P()),
        check_vma=False,
    )
```

```python
import functools
import math

import jax
import jax.numpy as jnp
from jax import lax
from jax.experimental import pallas as pl
from jax.experimental.pallas import tpu as pltpu
from jax.sharding import PartitionSpec as P

EPSILON = 1e-06
SOFTNESS_DIVISOR = 0.25
F32 = jnp.float32
BF16 = jnp.bfloat16
VMEM_LIMIT = 52 * 1024 * 1024
MANY = 4


def iota(shape, axis):
    return lax.broadcasted_iota(jnp.int32, shape, axis)


def contract(a, b, da, db):
    return lax.dot_general(a, b, (((da,), (db,)), ((), ())), preferred_element_type=F32)


def cost(micros):
    return pl.CostEstimate(flops=0, bytes_accessed=int(micros * 3.5e6), transcendentals=0)


def call(kernel, grid, in_specs, out_specs, out_shape, micros, scratch=()):
    return pl.pallas_call(
        kernel,
        grid=(grid,),
        in_specs=in_specs,
        out_specs=out_specs,
        out_shape=out_shape,
        scratch_shapes=list(scratch),
        compiler_params=pltpu.CompilerParams(vmem_limit_bytes=VMEM_LIMIT),
        cost_estimate=cost(micros),
    )


def whole(shape):
    return pl.BlockSpec(shape, lambda i: (0,) * len(shape))


def slab(cap, piece, many=1):
    return pl.BlockSpec((many, cap, piece), lambda i: (i, 0, 0))


def table_column(table_ref, index):
    lanes = iota(table_ref.shape, 1)
    return jnp.sum(jnp.where(lanes == index, table_ref[...], 0.0), axis=1, keepdims=True)


def add_column(table_ref, index, column):
    table_ref[...] += jnp.where(iota(table_ref.shape, 1) == index, column, 0.0)


def slot_value(pos, values, cap):
    match = iota((cap, pos.shape[1]), 0) == pos
    return jnp.sum(jnp.where(match, values, 0.0), axis=1, keepdims=True)


def slot_pick(pos, values, cap):
    slots = iota((cap, pos.shape[1]), 0).astype(F32).astype(BF16)
    return jnp.where(slots == pos.astype(F32).astype(BF16), values, jnp.zeros((), BF16))


def one_hot(match):
    return jnp.where(match, 1.0, 0.0).astype(BF16)


def tables_kernel(owner_ref, row_ref, pos_ref, code_ref):
    negs, rows = owner_ref.shape
    n_data = pos_ref.shape[0]
    ids = iota((n_data, rows), 0)
    asked = jnp.full((n_data, rows), -1, jnp.int32)
    for k in range(negs):
        asked = jnp.where(owner_ref[k : k + 1, :] == ids, row_ref[k : k + 1, :], asked)
    hit = one_hot(asked >= 0)
    before = one_hot(iota((rows, rows), 0) < iota((rows, rows), 1))
    count = contract(hit, before, 1, 0).astype(jnp.int32)
    pos_ref[...] = jnp.where(asked >= 0, count, -1)
    code_ref[...] = jnp.where(asked >= 0, asked * 1024 + count, -1).astype(F32)


def make_tables(owner_t, row_t, n_data):
    negs, rows = owner_t.shape
    return call(
        tables_kernel,
        1,
        [whole((negs, rows)), whole((negs, rows))],
        [whole((n_data, rows)), whole((n_data, rows))],
        [
            jax.ShapeDtypeStruct((n_data, rows), jnp.int32),
            jax.ShapeDtypeStruct((n_data, rows), F32),
        ],
        1,
    )(owner_t, row_t)


def decode(code_ref, index):
    code = code_ref[pl.ds(index, 1), :].astype(jnp.int32)
    return code & 1023, code >> 10


def serve_kernel(code_ref, p_ref, slot_ref, pick_ref):
    many, cap, piece = slot_ref.shape
    rows = p_ref.shape[0]
    for t in range(many):
        pos, asked = decode(code_ref, pl.program_id(0) * many + t)
        wanted = slot_value(pos, (asked + 1).astype(F32), cap).astype(jnp.int32) - 1
        pick_ref[t * cap : (t + 1) * cap, :] = one_hot(iota((cap, rows), 1) == wanted)
    found = contract(pick_ref[...], p_ref[...], 1, 0).astype(BF16)
    slot_ref[...] = found.reshape(many, cap, piece)


def serve(code, passages, cap):
    n_data, rows = code.shape
    piece = passages.shape[1]
    return call(
        serve_kernel,
        n_data // MANY,
        [whole((n_data, rows)), whole((rows, piece))],
        slab(cap, piece, MANY),
        jax.ShapeDtypeStruct((n_data, cap, piece), BF16),
        8,
        [pltpu.VMEM((MANY * cap, rows), BF16)],
    )(code, passages)


def match_kernel(code_ref, match_ref):
    rows = match_ref.shape[2]
    cap = match_ref.shape[1] // MANY
    for t in range(MANY):
        pos, asked = decode(code_ref, pl.program_id(0) * MANY + t)
        wanted = slot_value(pos, (asked + 1).astype(F32), cap).astype(jnp.int32) - 1
        match_ref[0, t * cap : (t + 1) * cap, :] = one_hot(iota((cap, rows), 1) == wanted)


def make_match(code, cap):
    n_data, rows = code.shape
    steps = n_data // MANY
    return call(
        match_kernel,
        steps,
        [whole((n_data, rows))],
        slab(MANY * cap, rows),
        jax.ShapeDtypeStruct((steps, MANY * cap, rows), BF16),
        8,
    )(code)


def slots_kernel(pos_ref, q_ref, inverse_ref, slot_ref, table_ref, pick_ref):
    step = pl.program_id(0)
    many, cap, piece = slot_ref.shape

    @pl.when(step == 0)
    def _():
        table_ref[...] = jnp.zeros_like(table_ref)

    for t in range(many):
        pos = pos_ref[pl.ds(step * many + t, 1), :]
        pick_ref[t * cap : (t + 1) * cap, :] = slot_pick(pos, jnp.ones((), BF16), cap)
        add_column(table_ref, step * many + t, slot_value(pos, inverse_ref[...], cap))
    found = contract(pick_ref[...], q_ref[...], 1, 0).astype(BF16)
    slot_ref[...] = found.reshape(many, cap, piece)


def make_slots(pos, q_emb, inverse, cap):
    n_data, rows = pos.shape
    piece = q_emb.shape[1]
    return call(
        slots_kernel,
        n_data // MANY,
        [whole((n_data, rows)), whole((rows, piece)), whole((1, rows))],
        [slab(cap, piece, MANY), whole((cap, n_data))],
        [
            jax.ShapeDtypeStruct((n_data, cap, piece), BF16),
            jax.ShapeDtypeStruct((cap, n_data), F32),
        ],
        9,
        [pltpu.VMEM((MANY * cap, rows), BF16)],
    )(pos, q_emb, inverse)


def collect_kernel(first, counts, base_ref, code_ref, *refs):
    q_refs, slot_ref = refs[:-1], refs[-1]
    step = pl.program_id(0)
    many, cap, _ = slot_ref.shape
    rows = code_ref.shape[1]

    def fill(q_ref, source):
        for t in range(many):
            pos, _ = decode(code_ref, source + t)
            pick = slot_pick(pos, jnp.ones((), BF16), cap)
            found = contract(pick, q_ref[t * rows : (t + 1) * rows, :], 1, 0)
            slot_ref[t] = found.astype(BF16)

    start = 0
    for place, count in enumerate(counts):
        source = base_ref[first + place] + (step - start) * many
        pl.when((step >= start) & (step < start + count))(
            functools.partial(fill, q_refs[place], source)
        )
        start += count


def collect(base, first, code, cap, parts):
    n_data, rows = code.shape
    piece = parts[0].shape[1]
    many = MANY
    counts = [part.shape[0] // (rows * many) for part in parts]
    starts = [sum(counts[:i]) for i in range(len(counts))]

    def spec(start, count):
        return pl.BlockSpec(
            (many * rows, piece), lambda i: (jnp.clip(i - start, 0, count - 1), 0)
        )

    steps = sum(counts)
    return call(
        functools.partial(collect_kernel, first, counts),
        steps,
        [
            pl.BlockSpec(memory_space=pltpu.SMEM),
            whole((n_data, rows)),
            *[spec(start, count) for start, count in zip(starts, counts)],
        ],
        slab(cap, piece, many),
        jax.ShapeDtypeStruct((steps * many, cap, piece), BF16),
        0.3 * steps * many,
    )(base, code, *parts)


def near_kernel(scale, pos_ref, owner_ref, q_ref, p_ref, near_ref):
    step = pl.program_id(0)
    many, cap, _ = q_ref.shape
    rows = pos_ref.shape[1]
    chunk = 48

    @pl.when(step == 0)
    def _():
        near_ref[...] = jnp.zeros_like(near_ref)

    for t in range(many):
        owner = step * many + t
        pos = pos_ref[pl.ds(owner, 1), :]
        spread = jnp.zeros((8, rows), F32)
        for start in range(0, cap, chunk):
            span = slice(start, start + chunk)
            product = q_ref[t, span, :].astype(F32) * p_ref[t, span, :].astype(F32)
            score = jnp.sum(product, axis=1, keepdims=True) * scale
            match = iota((chunk, rows), 0) + start == pos
            spread += jnp.sum(jnp.where(match, score, 0.0).reshape(chunk // 8, 8, rows), axis=0)
        spread = jnp.sum(spread, axis=0, keepdims=True)
        near_ref[...] += jnp.where(owner_ref[...] == owner, spread, 0.0)


def near_scores(scale, pos, owner_t, q_slots, p_slots):
    n_data, cap, piece = q_slots.shape
    negs, rows = owner_t.shape
    many = 2 * MANY
    return call(
        functools.partial(near_kernel, scale),
        n_data // many,
        [whole((n_data, rows)), whole((negs, rows)), slab(cap, piece, many), slab(cap, piece, many)],
        whole((negs, rows)),
        jax.ShapeDtypeStruct((negs, rows), F32),
        9,
    )(pos, owner_t, q_slots, p_slots)


def batch_kernel(scores_ref, stats_ref):
    scores = scores_ref[...]
    top = jnp.max(scores, axis=1, keepdims=True)
    total = jnp.sum(jnp.exp(scores - top), axis=1, keepdims=True)
    stats_ref[...] = jnp.where(iota(stats_ref.shape, 1) == 0, top, total)


def batch_stats(scores):
    share, rows = scores.shape
    return call(
        batch_kernel,
        1,
        [whole((share, rows))],
        whole((share, 2)),
        jax.ShapeDtypeStruct((share, 2), F32),
        1,
    )(scores)


def softmax_kernel(owner_ref, near_ref, stats_ref, hard_ref, lse_ref):
    near = jnp.sum(near_ref[...], axis=0)
    batch_top = stats_ref[0:1, :]
    top = jnp.maximum(batch_top, jnp.max(near, axis=0, keepdims=True))
    total = stats_ref[1:2, :] * jnp.exp(batch_top - top) + jnp.sum(
        jnp.exp(near - top), axis=0, keepdims=True
    )
    lse = top + jnp.log(total)
    lse_ref[...] = lse
    hard = jnp.exp(near - lse).astype(BF16).astype(F32)
    ids = iota(hard_ref.shape, 0)
    spread = jnp.zeros(hard_ref.shape, F32)
    for k in range(hard.shape[0]):
        spread += jnp.where(owner_ref[k : k + 1, :] == ids, hard[k : k + 1, :], 0.0)
    hard_ref[...] = spread


def softmax_all(owner_t, near, stats, n_data):
    n_members, negs, rows = near.shape
    return call(
        softmax_kernel,
        1,
        [whole((negs, rows)), whole((n_members, negs, rows)), whole((2, rows))],
        [whole((n_data, rows)), whole((1, rows))],
        [jax.ShapeDtypeStruct((n_data, rows), F32), jax.ShapeDtypeStruct((1, rows), F32)],
        2,
    )(owner_t, near, stats)


def weigh_kernel(pos_ref, hard_ref, table_ref):
    step = pl.program_id(0)
    many = 8

    @pl.when(step == 0)
    def _():
        table_ref[...] = jnp.zeros_like(table_ref)

    lanes = iota(table_ref.shape, 1)
    total = table_ref[...]
    for t in range(many):
        at = step * many + t
        weight = slot_value(pos_ref[pl.ds(at, 1), :], hard_ref[pl.ds(at, 1), :], total.shape[0])
        total = jnp.where(lanes == at, weight, total)
    table_ref[...] = total


def weigh_slots(pos, hard, cap):
    n_data, rows = pos.shape
    return call(
        weigh_kernel,
        n_data // 8,
        [whole((n_data, rows)), whole((n_data, rows))],
        whole((cap, n_data)),
        jax.ShapeDtypeStruct((cap, n_data), F32),
        5,
    )(pos, hard)


def hard_grad_kernel(scale, pos_ref, hard_ref, table_ref, q_ref, p_ref, total_ref, sum_ref, spread_ref):
    step = pl.program_id(0)
    many, cap, piece = p_ref.shape

    @pl.when(step == 0)
    def _():
        total_ref[...] = jnp.zeros_like(total_ref)
        sum_ref[...] = jnp.zeros_like(sum_ref)

    gain = jnp.zeros((8, piece), F32)
    for t in range(many):
        at = step * many + t
        hard = hard_ref[pl.ds(at, 1), :].astype(BF16)
        spread_ref[t * cap : (t + 1) * cap, :] = slot_pick(pos_ref[pl.ds(at, 1), :], hard, cap)
        weight = table_column(table_ref, at) * scale
        pairs = (weight * q_ref[t].astype(F32)).astype(BF16).astype(F32)
        gain += jnp.sum((pairs * p_ref[t].astype(F32)).reshape(cap // 8, 8, piece), axis=0)
    sum_ref[...] += jnp.sum(gain, axis=0, keepdims=True)
    total_ref[...] += contract(p_ref[...].reshape(many * cap, piece), spread_ref[...], 0, 0)


def hard_grad(scale, pos, hard, table, q_slots, p_slots):
    n_data, cap, piece = p_slots.shape
    rows = pos.shape[1]
    return call(
        functools.partial(hard_grad_kernel, scale),
        n_data // MANY,
        [
            whole((n_data, rows)),
            whole((n_data, rows)),
            whole((cap, n_data)),
            slab(cap, piece, MANY),
            slab(cap, piece, MANY),
        ],
        [whole((piece, rows)), whole((1, piece))],
        [jax.ShapeDtypeStruct((piece, rows), F32), jax.ShapeDtypeStruct((1, piece), F32)],
        12,
        [pltpu.VMEM((MANY * cap, rows), BF16)],
    )(pos, hard, table, q_slots, p_slots)


def pair_kernel(scale, spans, base_ref, table_ref, gain_ref, match_ref, other_ref, *refs):
    q_refs, (total_ref, pairs_ref, split_ref) = refs[: len(spans)], refs[len(spans) :]
    step = pl.program_id(0)
    many, cap, piece = q_refs[0].shape
    deep = match_ref.shape[1]
    wide = table_ref.shape[1]
    n_data = wide // 4

    @pl.when(step == 0)
    def _():
        total_ref[...] = jnp.zeros_like(total_ref)
        table = table_ref[...]
        high = table.astype(BF16).astype(F32)
        middle = (table - high).astype(BF16).astype(F32)
        low = table - high - middle
        place = iota(table.shape, 1) // n_data
        split = jnp.where(place == 3, low, jnp.where(place == 2, middle, high))
        split_ref[...] = split.astype(BF16)

    lane = iota((wide, many * 128), 0)
    place = iota((wide, many * 128), 1) // 128
    half = many // 2
    wanted = jnp.where(place < half, base_ref[2 * step] + place, base_ref[2 * step + 1] + place - half)
    weights = contract(split_ref[...], one_hot(lane == wanted), 1, 0) * scale
    spread = (lane >= n_data) & (lane % n_data == wanted)
    inverses = contract(split_ref[...], one_hot(spread), 1, 0)

    def fill(q_ref):
        for t in range(many):
            for lanes in range(0, piece, 128):
                span = slice(lanes, lanes + 128)
                raw = q_ref[t, :, span].astype(F32)
                column = slice(t * 128, (t + 1) * 128)
                emb = ((raw * inverses[:, column]) * gain_ref[:, span]).astype(BF16)
                pairs = (weights[:, column] * emb.astype(F32)).astype(BF16)
                pairs_ref[t * cap : (t + 1) * cap, span] = pairs

    for place, (low, high) in enumerate(spans):
        pl.when((step >= low) & (step < high))(functools.partial(fill, q_refs[place]))
    total = contract(pairs_ref[:deep, :], match_ref[0], 0, 0)
    total_ref[...] += total + contract(pairs_ref[deep:, :], other_ref[0], 0, 0)


def pair_grad(scale, base, table, gain, match, parts):
    cap, wide = table.shape
    groups, deep, rows = match.shape
    piece = parts[0].shape[2]
    steps, each = groups // 2, wide // 4 // groups
    many = 2 * each
    ends = [sum(part.shape[0] for part in parts[: i + 1]) // many for i in range(len(parts))]
    spans = list(zip([0] + ends[:-1], ends))

    def part_spec(span):
        low, high = span
        return pl.BlockSpec(
            (many, cap, piece), lambda i, base_ref: (jnp.clip(i, low, high - 1) - low, 0, 0)
        )

    return pl.pallas_call(
        functools.partial(pair_kernel, scale, spans),
        grid_spec=pltpu.PrefetchScalarGridSpec(
            num_scalar_prefetch=1,
            grid=(steps,),
            in_specs=[
                pl.BlockSpec((cap, wide), lambda i, base_ref: (0, 0)),
                pl.BlockSpec((1, piece), lambda i, base_ref: (0, 0)),
                pl.BlockSpec((1, deep, rows), lambda i, base_ref: (base_ref[2 * i] // each, 0, 0)),
                pl.BlockSpec((1, deep, rows), lambda i, base_ref: (base_ref[2 * i + 1] // each, 0, 0)),
                *[part_spec(span) for span in spans],
            ],
            out_specs=pl.BlockSpec((piece, rows), lambda i, base_ref: (0, 0)),
            scratch_shapes=[pltpu.VMEM((2 * deep, piece), BF16), pltpu.VMEM((cap, wide), BF16)],
        ),
        out_shape=jax.ShapeDtypeStruct((piece, rows), F32),
        compiler_params=pltpu.CompilerParams(vmem_limit_bytes=VMEM_LIMIT),
        cost_estimate=cost(10),
    )(base, table, gain, match, match, *parts)


def swap(x, axis):
    return lax.all_to_all(x, axis, split_axis=0, concat_axis=0, tiled=True)


def tied(*values):
    return lax.optimization_barrier(values)


class Torus:
    def __init__(self, n_data, nx):
        self.nx, self.nz = nx, n_data // nx
        self.along_z = [[x * self.nz + z for z in range(self.nz)] for x in range(nx)]

    def shift(self, value, by):
        nx, nz = self.nx, self.nz
        pairs = [
            (x * nz + z, (x + by) % nx * nz + z) for x in range(nx) for z in range(nz)
        ]
        return lax.ppermute(value, "dp", pairs)

    def gather_z(self, value):
        return lax.all_gather(value, "dp", axis=0, tiled=True, axis_index_groups=self.along_z)


def local(nx, queries, passages, neg_owner, neg_row, gain):
    rows, piece = queries.shape
    negs = neg_owner.shape[1]
    n_data = lax.axis_size("dp")
    n_members = lax.axis_size("group")
    member = lax.axis_index("group")
    width = piece * n_members
    cap = min(rows, 5 * rows * negs // (4 * n_data))
    scale = 1.0 / (SOFTNESS_DIVISOR * math.sqrt(width))
    torus = Torus(n_data, nx)
    nz = torus.nz
    my_x = (lax.axis_index("dp") // nz).astype(jnp.int32)
    my_gain = lax.dynamic_slice_in_dim(gain, member * piece, piece, 0)
    gain_row = my_gain[None, :]
    owner_t = neg_owner.T

    away = jnp.array([0, 0, 3, 1, 1, 3, 2, 2], jnp.int32)
    upper = jnp.array([0, 1, 0, 1, 0, 1, 0, 1], jnp.int32)
    base = (my_x + away) % nx * nz + upper * (nz // 2)

    q_zero = torus.gather_z(queries)
    half = q_zero.shape[0] // 2

    pos, code = make_tables(owner_t, neg_row.T, n_data)

    q_values = queries.astype(F32)
    p_values = passages.astype(F32)
    squares = jnp.stack(
        [jnp.sum(q_values * q_values, axis=1), jnp.sum(p_values * p_values, axis=1)]
    )
    squares = swap(jnp.broadcast_to(squares.reshape(1, -1), (n_members, 2 * rows)), "group")
    squares = jnp.sum(squares, axis=0).reshape(2, rows)
    squares, code = tied(squares, code)
    code_got = swap(code, "dp")
    inverses = lax.rsqrt(squares / width + EPSILON)
    q_inverse, p_inverse = inverses[0][:, None], inverses[1][:, None]
    q_normed = q_values * q_inverse
    p_normed = p_values * p_inverse
    q_emb = (q_normed * my_gain).astype(BF16)
    p_emb = (p_normed * my_gain).astype(BF16)
    p_slots = swap(serve(code_got, p_emb, cap), "dp")

    scores = contract(q_emb, p_emb, 1, 1) * scale
    scores = lax.psum_scatter(scores, "group", scatter_dimension=0, tiled=True)
    q_slots, inverse = make_slots(pos, q_emb, inverses[:1], cap)
    match = make_match(code_got, cap)
    q_lower, q_upper = q_zero[:half], q_zero[half:]
    q_three_low, q_one_high = torus.shift(q_lower, 1), torus.shift(q_upper, -1)
    part_zero = collect(base, 0, code_got, cap, [q_zero])
    scores, q_slots, match, q_three_low, q_one_high, q_lower, q_upper, part_zero = tied(
        scores, q_slots, match, q_three_low, q_one_high, q_lower, q_upper, part_zero
    )
    stats = batch_stats(scores)
    scores = lax.all_gather(scores, "group", axis=0, tiled=True)
    q_one_low, q_three_high = torus.shift(q_lower, -1), torus.shift(q_upper, 1)
    q_low, q_high = torus.shift(q_three_low, 1), torus.shift(q_one_high, -1)
    part_first = collect(base, 2, code_got, cap, [q_three_low, q_one_high])
    p_slots, stats, part_first = tied(p_slots, stats, part_first)

    near = near_scores(scale, pos, owner_t, q_slots, p_slots)
    share = rows // n_members
    per = 2 * share // negs
    stats = jnp.pad(stats.T.reshape(negs, per), ((0, 0), (0, -per % 128)))
    mixed = lax.all_gather(jnp.concatenate([near, stats], axis=1), "group", axis=0)
    near = mixed[:, :, :rows]
    stats = mixed[:, :, rows : rows + per].reshape(n_members, 2, share)
    stats = stats.transpose(1, 0, 2).reshape(2, rows)
    hard, lse = softmax_all(owner_t, near, stats, n_data)
    table = weigh_slots(pos, hard, cap)
    hard_q, pair_gain = hard_grad(scale, pos, hard, table, q_slots, p_slots)
    lse = lse[0][:, None]
    positive = iota((rows, rows), 0) == iota((rows, rows), 1)
    weights = (jnp.exp(scores - lse) - positive.astype(F32)).astype(BF16)
    losses = jnp.sum(lse) - jnp.sum(jnp.where(positive, scores, 0.0))
    grad_q = (contract(weights, p_emb, 1, 0) + hard_q.T) * scale
    batch_grad = contract(weights, q_emb, 0, 0) * scale
    gain_part = (
        jnp.sum(grad_q * q_normed, axis=0)
        + jnp.sum(batch_grad * p_normed, axis=0)
        + pair_gain[0] / my_gain
    )
    last = jnp.concatenate([gain_part, jnp.broadcast_to(losses, (128,))])
    _, q_one_low, q_three_high, q_low, q_high = tied(last, q_one_low, q_three_high, q_low, q_high)
    sent = jnp.concatenate([table, inverse, jnp.zeros((-2 * cap % 128, n_data), F32)], axis=0).T
    edge = sent.shape[1]
    sent = jnp.concatenate([sent, jnp.broadcast_to(last[None, :], (n_data, piece + 128))], axis=1)
    got = swap(sent, "dp")
    last = jnp.sum(got[:, edge:], axis=0)
    got_weights, got_inverses = got[:, :cap].T, got[:, cap : 2 * cap].T
    table = jnp.concatenate([got_weights] + [got_inverses] * 3, axis=1)

    part_last = collect(base, 4, code_got, cap, [q_one_low, q_three_high, q_low, q_high])
    parts = [part_zero, part_first, part_last]
    grad_p = batch_grad + pair_grad(scale, base, table, gain_row, match, parts).T
    q_inner = grad_q * my_gain
    p_inner = grad_p * my_gain
    final = jnp.concatenate(
        [jnp.sum(q_inner * q_normed, axis=1), jnp.sum(p_inner * p_normed, axis=1), last]
    )
    final = swap(jnp.broadcast_to(final[None, :], (n_members, final.shape[0])), "group")
    means = jnp.sum(final[:, : 2 * rows], axis=0) / width
    q_mean, p_mean = means[:rows, None], means[rows:, None]
    grad_queries = (q_inverse * (q_inner - q_normed * q_mean)).astype(BF16)
    grad_passages = (p_inverse * (p_inner - p_normed * p_mean)).astype(BF16)
    count = rows * n_data
    grad_gain = final[:, 2 * rows : 2 * rows + piece].reshape(-1) / math.sqrt(count)
    loss = final[0, 2 * rows + piece] / count
    return grad_queries, grad_passages, grad_gain, loss


def solution(mesh):
    nx = 4
    return jax.shard_map(
        functools.partial(local, nx),
        mesh=mesh,
        in_specs=(P("dp", "group"), P("dp", "group"), P("dp", None), P("dp", None), P()),
        out_specs=(P("dp", "group"), P("dp", "group"), P(), P()),
        check_vma=False,
    )
```

```python
import functools
import math

import jax
import jax.numpy as jnp
from jax import lax
from jax.experimental import pallas as pl
from jax.experimental.pallas import tpu as pltpu
from jax.sharding import PartitionSpec as P

EPSILON = 1e-06
SOFTNESS_DIVISOR = 0.25
F32 = jnp.float32
BF16 = jnp.bfloat16
VMEM_LIMIT = 52 * 1024 * 1024
MANY = 4


def iota(shape, axis):
    return lax.broadcasted_iota(jnp.int32, shape, axis)


def contract(a, b, da, db):
    return lax.dot_general(a, b, (((da,), (db,)), ((), ())), preferred_element_type=F32)


def cost(micros):
    return pl.CostEstimate(flops=0, bytes_accessed=int(micros * 3.5e6), transcendentals=0)


def call(kernel, grid, in_specs, out_specs, out_shape, micros, scratch=()):
    return pl.pallas_call(
        kernel,
        grid=(grid,),
        in_specs=in_specs,
        out_specs=out_specs,
        out_shape=out_shape,
        scratch_shapes=list(scratch),
        compiler_params=pltpu.CompilerParams(vmem_limit_bytes=VMEM_LIMIT),
        cost_estimate=cost(micros),
    )


def whole(shape):
    return pl.BlockSpec(shape, lambda i: (0,) * len(shape))


def slab(cap, piece, many=1):
    return pl.BlockSpec((many, cap, piece), lambda i: (i, 0, 0))


def table_column(table_ref, index):
    lanes = iota(table_ref.shape, 1)
    return jnp.sum(jnp.where(lanes == index, table_ref[...], 0.0), axis=1, keepdims=True)


def add_column(table_ref, index, column):
    table_ref[...] += jnp.where(iota(table_ref.shape, 1) == index, column, 0.0)


def slot_value(pos, values, cap):
    match = iota((cap, pos.shape[1]), 0) == pos
    return jnp.sum(jnp.where(match, values, 0.0), axis=1, keepdims=True)


def slot_pick(pos, values, cap):
    slots = iota((cap, pos.shape[1]), 0).astype(F32).astype(BF16)
    return jnp.where(slots == pos.astype(F32).astype(BF16), values, jnp.zeros((), BF16))


def one_hot(match):
    return jnp.where(match, 1.0, 0.0).astype(BF16)


def tables_kernel(owner_ref, row_ref, pos_ref, code_ref):
    negs, rows = owner_ref.shape
    n_data = pos_ref.shape[0]
    ids = iota((n_data, rows), 0)
    asked = jnp.full((n_data, rows), -1, jnp.int32)
    for k in range(negs):
        asked = jnp.where(owner_ref[k : k + 1, :] == ids, row_ref[k : k + 1, :], asked)
    hit = one_hot(asked >= 0)
    before = one_hot(iota((rows, rows), 0) < iota((rows, rows), 1))
    count = contract(hit, before, 1, 0).astype(jnp.int32)
    pos_ref[...] = jnp.where(asked >= 0, count, -1)
    code_ref[...] = jnp.where(asked >= 0, asked * 1024 + count, -1).astype(F32)


def make_tables(owner_t, row_t, n_data):
    negs, rows = owner_t.shape
    return call(
        tables_kernel,
        1,
        [whole((negs, rows)), whole((negs, rows))],
        [whole((n_data, rows)), whole((n_data, rows))],
        [
            jax.ShapeDtypeStruct((n_data, rows), jnp.int32),
            jax.ShapeDtypeStruct((n_data, rows), F32),
        ],
        1,
    )(owner_t, row_t)


def decode(code_ref, index):
    code = code_ref[pl.ds(index, 1), :].astype(jnp.int32)
    return code & 1023, code >> 10


def serve_kernel(code_ref, p_ref, slot_ref, pick_ref):
    many, cap, piece = slot_ref.shape
    rows = p_ref.shape[0]
    for t in range(many):
        pos, asked = decode(code_ref, pl.program_id(0) * many + t)
        wanted = slot_value(pos, (asked + 1).astype(F32), cap).astype(jnp.int32) - 1
        pick_ref[t * cap : (t + 1) * cap, :] = one_hot(iota((cap, rows), 1) == wanted)
    found = contract(pick_ref[...], p_ref[...], 1, 0).astype(BF16)
    slot_ref[...] = found.reshape(many, cap, piece)


def serve(code, passages, cap):
    n_data, rows = code.shape
    piece = passages.shape[1]
    return call(
        serve_kernel,
        n_data // MANY,
        [whole((n_data, rows)), whole((rows, piece))],
        slab(cap, piece, MANY),
        jax.ShapeDtypeStruct((n_data, cap, piece), BF16),
        8,
        [pltpu.VMEM((MANY * cap, rows), BF16)],
    )(code, passages)


def match_kernel(code_ref, match_ref):
    rows = match_ref.shape[2]
    cap = match_ref.shape[1] // MANY
    for t in range(MANY):
        pos, asked = decode(code_ref, pl.program_id(0) * MANY + t)
        wanted = slot_value(pos, (asked + 1).astype(F32), cap).astype(jnp.int32) - 1
        match_ref[0, t * cap : (t + 1) * cap, :] = one_hot(iota((cap, rows), 1) == wanted)


def make_match(code, cap):
    n_data, rows = code.shape
    steps = n_data // MANY
    return call(
        match_kernel,
        steps,
        [whole((n_data, rows))],
        slab(MANY * cap, rows),
        jax.ShapeDtypeStruct((steps, MANY * cap, rows), BF16),
        8,
    )(code)


def slots_kernel(pos_ref, q_ref, inverse_ref, slot_ref, table_ref, pick_ref):
    step = pl.program_id(0)
    many, cap, piece = slot_ref.shape

    @pl.when(step == 0)
    def _():
        table_ref[...] = jnp.zeros_like(table_ref)

    for t in range(many):
        pos = pos_ref[pl.ds(step * many + t, 1), :]
        pick_ref[t * cap : (t + 1) * cap, :] = slot_pick(pos, jnp.ones((), BF16), cap)
        add_column(table_ref, step * many + t, slot_value(pos, inverse_ref[...], cap))
    found = contract(pick_ref[...], q_ref[...], 1, 0).astype(BF16)
    slot_ref[...] = found.reshape(many, cap, piece)


def make_slots(pos, q_emb, inverse, cap):
    n_data, rows = pos.shape
    piece = q_emb.shape[1]
    return call(
        slots_kernel,
        n_data // MANY,
        [whole((n_data, rows)), whole((rows, piece)), whole((1, rows))],
        [slab(cap, piece, MANY), whole((cap, n_data))],
        [
            jax.ShapeDtypeStruct((n_data, cap, piece), BF16),
            jax.ShapeDtypeStruct((cap, n_data), F32),
        ],
        9,
        [pltpu.VMEM((MANY * cap, rows), BF16)],
    )(pos, q_emb, inverse)


def collect_kernel(first, counts, base_ref, code_ref, *refs):
    q_refs, slot_ref = refs[:-1], refs[-1]
    step = pl.program_id(0)
    many, cap, _ = slot_ref.shape
    rows = code_ref.shape[1]

    def fill(q_ref, source):
        for t in range(many):
            pos, _ = decode(code_ref, source + t)
            pick = slot_pick(pos, jnp.ones((), BF16), cap)
            found = contract(pick, q_ref[t * rows : (t + 1) * rows, :], 1, 0)
            slot_ref[t] = found.astype(BF16)

    start = 0
    for place, count in enumerate(counts):
        source = base_ref[first + place] + (step - start) * many
        pl.when((step >= start) & (step < start + count))(
            functools.partial(fill, q_refs[place], source)
        )
        start += count


def collect(base, first, code, cap, parts):
    n_data, rows = code.shape
    piece = parts[0].shape[1]
    many = MANY
    counts = [part.shape[0] // (rows * many) for part in parts]
    starts = [sum(counts[:i]) for i in range(len(counts))]

    def spec(start, count):
        return pl.BlockSpec(
            (many * rows, piece), lambda i: (jnp.clip(i - start, 0, count - 1), 0)
        )

    steps = sum(counts)
    return call(
        functools.partial(collect_kernel, first, counts),
        steps,
        [
            pl.BlockSpec(memory_space=pltpu.SMEM),
            whole((n_data, rows)),
            *[spec(start, count) for start, count in zip(starts, counts)],
        ],
        slab(cap, piece, many),
        jax.ShapeDtypeStruct((steps * many, cap, piece), BF16),
        0.3 * steps * many,
    )(base, code, *parts)


def near_kernel(scale, pos_ref, owner_ref, q_ref, p_ref, near_ref):
    step = pl.program_id(0)
    many, cap, _ = q_ref.shape
    rows = pos_ref.shape[1]
    chunk = 48

    @pl.when(step == 0)
    def _():
        near_ref[...] = jnp.zeros_like(near_ref)

    for t in range(many):
        owner = step * many + t
        pos = pos_ref[pl.ds(owner, 1), :]
        spread = jnp.zeros((8, rows), F32)
        for start in range(0, cap, chunk):
            span = slice(start, start + chunk)
            product = q_ref[t, span, :].astype(F32) * p_ref[t, span, :].astype(F32)
            score = jnp.sum(product, axis=1, keepdims=True) * scale
            match = iota((chunk, rows), 0) + start == pos
            spread += jnp.sum(jnp.where(match, score, 0.0).reshape(chunk // 8, 8, rows), axis=0)
        spread = jnp.sum(spread, axis=0, keepdims=True)
        near_ref[...] += jnp.where(owner_ref[...] == owner, spread, 0.0)


def near_scores(scale, pos, owner_t, q_slots, p_slots):
    n_data, cap, piece = q_slots.shape
    negs, rows = owner_t.shape
    many = 2 * MANY
    return call(
        functools.partial(near_kernel, scale),
        n_data // many,
        [whole((n_data, rows)), whole((negs, rows)), slab(cap, piece, many), slab(cap, piece, many)],
        whole((negs, rows)),
        jax.ShapeDtypeStruct((negs, rows), F32),
        9,
    )(pos, owner_t, q_slots, p_slots)


def batch_kernel(scores_ref, stats_ref):
    scores = scores_ref[...]
    top = jnp.max(scores, axis=1, keepdims=True)
    total = jnp.sum(jnp.exp(scores - top), axis=1, keepdims=True)
    stats_ref[...] = jnp.where(iota(stats_ref.shape, 1) == 0, top, total)


def batch_stats(scores):
    share, rows = scores.shape
    return call(
        batch_kernel,
        1,
        [whole((share, rows))],
        whole((share, 2)),
        jax.ShapeDtypeStruct((share, 2), F32),
        1,
    )(scores)


def softmax_kernel(owner_ref, near_ref, stats_ref, hard_ref, lse_ref):
    near = jnp.sum(near_ref[...], axis=0)
    batch_top = stats_ref[0:1, :]
    top = jnp.maximum(batch_top, jnp.max(near, axis=0, keepdims=True))
    total = stats_ref[1:2, :] * jnp.exp(batch_top - top) + jnp.sum(
        jnp.exp(near - top), axis=0, keepdims=True
    )
    lse = top + jnp.log(total)
    lse_ref[...] = lse
    hard = jnp.exp(near - lse).astype(BF16).astype(F32)
    ids = iota(hard_ref.shape, 0)
    spread = jnp.zeros(hard_ref.shape, F32)
    for k in range(hard.shape[0]):
        spread += jnp.where(owner_ref[k : k + 1, :] == ids, hard[k : k + 1, :], 0.0)
    hard_ref[...] = spread


def softmax_all(owner_t, near, stats, n_data):
    n_members, negs, rows = near.shape
    return call(
        softmax_kernel,
        1,
        [whole((negs, rows)), whole((n_members, negs, rows)), whole((2, rows))],
        [whole((n_data, rows)), whole((1, rows))],
        [jax.ShapeDtypeStruct((n_data, rows), F32), jax.ShapeDtypeStruct((1, rows), F32)],
        2,
    )(owner_t, near, stats)


def weigh_kernel(pos_ref, hard_ref, table_ref):
    step = pl.program_id(0)
    many = 8

    @pl.when(step == 0)
    def _():
        table_ref[...] = jnp.zeros_like(table_ref)

    lanes = iota(table_ref.shape, 1)
    total = table_ref[...]
    for t in range(many):
        at = step * many + t
        weight = slot_value(pos_ref[pl.ds(at, 1), :], hard_ref[pl.ds(at, 1), :], total.shape[0])
        total = jnp.where(lanes == at, weight, total)
    table_ref[...] = total


def weigh_slots(pos, hard, cap):
    n_data, rows = pos.shape
    return call(
        weigh_kernel,
        n_data // 8,
        [whole((n_data, rows)), whole((n_data, rows))],
        whole((cap, n_data)),
        jax.ShapeDtypeStruct((cap, n_data), F32),
        5,
    )(pos, hard)


def hard_grad_kernel(scale, pos_ref, hard_ref, table_ref, q_ref, p_ref, total_ref, sum_ref, spread_ref):
    step = pl.program_id(0)
    many, cap, piece = p_ref.shape

    @pl.when(step == 0)
    def _():
        total_ref[...] = jnp.zeros_like(total_ref)
        sum_ref[...] = jnp.zeros_like(sum_ref)

    gain = jnp.zeros((8, piece), F32)
    for t in range(many):
        at = step * many + t
        hard = hard_ref[pl.ds(at, 1), :].astype(BF16)
        spread_ref[t * cap : (t + 1) * cap, :] = slot_pick(pos_ref[pl.ds(at, 1), :], hard, cap)
        weight = table_column(table_ref, at) * scale
        pairs = (weight * q_ref[t].astype(F32)).astype(BF16).astype(F32)
        gain += jnp.sum((pairs * p_ref[t].astype(F32)).reshape(cap // 8, 8, piece), axis=0)
    sum_ref[...] += jnp.sum(gain, axis=0, keepdims=True)
    total_ref[...] += contract(p_ref[...].reshape(many * cap, piece), spread_ref[...], 0, 0)


def hard_grad(scale, pos, hard, table, q_slots, p_slots):
    n_data, cap, piece = p_slots.shape
    rows = pos.shape[1]
    return call(
        functools.partial(hard_grad_kernel, scale),
        n_data // MANY,
        [
            whole((n_data, rows)),
            whole((n_data, rows)),
            whole((cap, n_data)),
            slab(cap, piece, MANY),
            slab(cap, piece, MANY),
        ],
        [whole((piece, rows)), whole((1, piece))],
        [jax.ShapeDtypeStruct((piece, rows), F32), jax.ShapeDtypeStruct((1, piece), F32)],
        12,
        [pltpu.VMEM((MANY * cap, rows), BF16)],
    )(pos, hard, table, q_slots, p_slots)


def pair_kernel(scale, spans, base_ref, table_ref, gain_ref, match_ref, other_ref, *refs):
    q_refs, (total_ref, pairs_ref, split_ref) = refs[: len(spans)], refs[len(spans) :]
    step = pl.program_id(0)
    many, cap, piece = q_refs[0].shape
    deep = match_ref.shape[1]
    wide = table_ref.shape[1]
    n_data = wide // 4

    @pl.when(step == 0)
    def _():
        total_ref[...] = jnp.zeros_like(total_ref)
        table = table_ref[...]
        high = table.astype(BF16).astype(F32)
        middle = (table - high).astype(BF16).astype(F32)
        low = table - high - middle
        place = iota(table.shape, 1) // n_data
        split = jnp.where(place == 3, low, jnp.where(place == 2, middle, high))
        split_ref[...] = split.astype(BF16)

    lane = iota((wide, many * 128), 0)
    place = iota((wide, many * 128), 1) // 128
    half = many // 2
    wanted = jnp.where(place < half, base_ref[2 * step] + place, base_ref[2 * step + 1] + place - half)
    weights = contract(split_ref[...], one_hot(lane == wanted), 1, 0) * scale
    spread = (lane >= n_data) & (lane % n_data == wanted)
    inverses = contract(split_ref[...], one_hot(spread), 1, 0)

    def fill(q_ref):
        for t in range(many):
            for lanes in range(0, piece, 128):
                span = slice(lanes, lanes + 128)
                raw = q_ref[t, :, span].astype(F32)
                column = slice(t * 128, (t + 1) * 128)
                emb = ((raw * inverses[:, column]) * gain_ref[:, span]).astype(BF16)
                pairs = (weights[:, column] * emb.astype(F32)).astype(BF16)
                pairs_ref[t * cap : (t + 1) * cap, span] = pairs

    for place, (low, high) in enumerate(spans):
        pl.when((step >= low) & (step < high))(functools.partial(fill, q_refs[place]))
    total = contract(pairs_ref[:deep, :], match_ref[0], 0, 0)
    total_ref[...] += total + contract(pairs_ref[deep:, :], other_ref[0], 0, 0)


def pair_grad(scale, base, table, gain, match, parts):
    cap, wide = table.shape
    groups, deep, rows = match.shape
    piece = parts[0].shape[2]
    steps, each = groups // 2, wide // 4 // groups
    many = 2 * each
    ends = [sum(part.shape[0] for part in parts[: i + 1]) // many for i in range(len(parts))]
    spans = list(zip([0] + ends[:-1], ends))

    def part_spec(span):
        low, high = span
        return pl.BlockSpec(
            (many, cap, piece), lambda i, base_ref: (jnp.clip(i, low, high - 1) - low, 0, 0)
        )

    return pl.pallas_call(
        functools.partial(pair_kernel, scale, spans),
        grid_spec=pltpu.PrefetchScalarGridSpec(
            num_scalar_prefetch=1,
            grid=(steps,),
            in_specs=[
                pl.BlockSpec((cap, wide), lambda i, base_ref: (0, 0)),
                pl.BlockSpec((1, piece), lambda i, base_ref: (0, 0)),
                pl.BlockSpec((1, deep, rows), lambda i, base_ref: (base_ref[2 * i] // each, 0, 0)),
                pl.BlockSpec((1, deep, rows), lambda i, base_ref: (base_ref[2 * i + 1] // each, 0, 0)),
                *[part_spec(span) for span in spans],
            ],
            out_specs=pl.BlockSpec((piece, rows), lambda i, base_ref: (0, 0)),
            scratch_shapes=[pltpu.VMEM((2 * deep, piece), BF16), pltpu.VMEM((cap, wide), BF16)],
        ),
        out_shape=jax.ShapeDtypeStruct((piece, rows), F32),
        compiler_params=pltpu.CompilerParams(vmem_limit_bytes=VMEM_LIMIT),
        cost_estimate=cost(10),
    )(base, table, gain, match, match, *parts)


def swap(x, axis):
    return lax.all_to_all(x, axis, split_axis=0, concat_axis=0, tiled=True)


def tied(*values):
    return lax.optimization_barrier(values)


class Torus:
    def __init__(self, n_data, nx):
        self.nx, self.nz = nx, n_data // nx
        self.along_z = [[x * self.nz + z for z in range(self.nz)] for x in range(nx)]

    def shift(self, value, by):
        nx, nz = self.nx, self.nz
        pairs = [
            (x * nz + z, (x + by) % nx * nz + z) for x in range(nx) for z in range(nz)
        ]
        return lax.ppermute(value, "dp", pairs)

    def gather_z(self, value):
        return lax.all_gather(value, "dp", axis=0, tiled=True, axis_index_groups=self.along_z)


def local(nx, queries, passages, neg_owner, neg_row, gain):
    rows, piece = queries.shape
    negs = neg_owner.shape[1]
    n_data = lax.axis_size("dp")
    n_members = lax.axis_size("group")
    member = lax.axis_index("group")
    width = piece * n_members
    cap = min(rows, 5 * rows * negs // (4 * n_data))
    scale = 1.0 / (SOFTNESS_DIVISOR * math.sqrt(width))
    torus = Torus(n_data, nx)
    nz = torus.nz
    my_x = (lax.axis_index("dp") // nz).astype(jnp.int32)
    my_gain = lax.dynamic_slice_in_dim(gain, member * piece, piece, 0)
    gain_row = my_gain[None, :]
    owner_t = neg_owner.T

    away = jnp.array([0, 0, 3, 1, 1, 3, 2, 2], jnp.int32)
    upper = jnp.array([0, 1, 0, 1, 0, 1, 0, 1], jnp.int32)
    base = (my_x + away) % nx * nz + upper * (nz // 2)

    q_zero = torus.gather_z(queries)
    half = q_zero.shape[0] // 2

    pos, code = make_tables(owner_t, neg_row.T, n_data)
    code_got = swap(code, "dp")

    q_values = queries.astype(F32)
    p_values = passages.astype(F32)
    squares = jnp.stack(
        [jnp.sum(q_values * q_values, axis=1), jnp.sum(p_values * p_values, axis=1)]
    )
    squares = jnp.sum(lax.all_gather(squares, "group", axis=0), axis=0)
    squares, code_got = tied(squares, code_got)
    inverses = lax.rsqrt(squares / width + EPSILON)
    q_inverse, p_inverse = inverses[0][:, None], inverses[1][:, None]
    q_normed = q_values * q_inverse
    p_normed = p_values * p_inverse
    q_emb = (q_normed * my_gain).astype(BF16)
    p_emb = (p_normed * my_gain).astype(BF16)
    p_slots = swap(serve(code_got, p_emb, cap), "dp")

    scores = contract(q_emb, p_emb, 1, 1) * scale
    scores = lax.psum_scatter(scores, "group", scatter_dimension=0, tiled=True)
    q_slots, inverse = make_slots(pos, q_emb, inverses[:1], cap)
    match = make_match(code_got, cap)
    q_lower, q_upper = q_zero[:half], q_zero[half:]
    q_three_low, q_one_high = torus.shift(q_lower, 1), torus.shift(q_upper, -1)
    part_zero = collect(base, 0, code_got, cap, [q_zero])
    scores, q_slots, match, q_three_low, q_one_high, q_lower, q_upper, part_zero = tied(
        scores, q_slots, match, q_three_low, q_one_high, q_lower, q_upper, part_zero
    )
    stats = batch_stats(scores)
    scores = lax.all_gather(scores, "group", axis=0, tiled=True)
    q_one_low, q_three_high = torus.shift(q_lower, -1), torus.shift(q_upper, 1)
    q_low, q_high = torus.shift(q_three_low, 1), torus.shift(q_one_high, -1)
    p_slots, stats = tied(p_slots, stats)

    near = near_scores(scale, pos, owner_t, q_slots, p_slots)
    share = rows // n_members
    per = 2 * share // negs
    stats = jnp.pad(stats.T.reshape(negs, per), ((0, 0), (0, -per % 128)))
    mixed = lax.all_gather(jnp.concatenate([near, stats], axis=1), "group", axis=0)
    near = mixed[:, :, :rows]
    stats = mixed[:, :, rows : rows + per].reshape(n_members, 2, share)
    stats = stats.transpose(1, 0, 2).reshape(2, rows)
    hard, lse = softmax_all(owner_t, near, stats, n_data)
    table = weigh_slots(pos, hard, cap)
    hard_q, pair_gain = hard_grad(scale, pos, hard, table, q_slots, p_slots)
    lse = lse[0][:, None]
    positive = iota((rows, rows), 0) == iota((rows, rows), 1)
    weights = (jnp.exp(scores - lse) - positive.astype(F32)).astype(BF16)
    losses = jnp.sum(lse) - jnp.sum(jnp.where(positive, scores, 0.0))
    grad_q = (contract(weights, p_emb, 1, 0) + hard_q.T) * scale
    batch_grad = contract(weights, q_emb, 0, 0) * scale
    gain_part = (
        jnp.sum(grad_q * q_normed, axis=0)
        + jnp.sum(batch_grad * p_normed, axis=0)
        + pair_gain[0] / my_gain
    )
    last = jnp.concatenate([gain_part, jnp.broadcast_to(losses, (128,))])
    _, q_three_low, q_one_high, q_one_low, q_three_high = tied(
        last, q_three_low, q_one_high, q_one_low, q_three_high
    )
    sent = jnp.concatenate([table, inverse, jnp.zeros((-2 * cap % 128, n_data), F32)], axis=0).T
    edge = sent.shape[1]
    sent = jnp.concatenate([sent, jnp.broadcast_to(last[None, :], (n_data, piece + 128))], axis=1)
    got = swap(sent, "dp")
    last = jnp.sum(got[:, edge:], axis=0)
    got_weights, got_inverses = got[:, :cap].T, got[:, cap : 2 * cap].T
    table = jnp.concatenate([got_weights] + [got_inverses] * 3, axis=1)

    part_next = collect(
        base, 2, code_got, cap, [q_three_low, q_one_high, q_one_low, q_three_high]
    )
    part_next, q_low, q_high = tied(part_next, q_low, q_high)
    part_last = collect(base, 6, code_got, cap, [q_low, q_high])
    parts = [part_zero, part_next, part_last]
    grad_p = batch_grad + pair_grad(scale, base, table, gain_row, match, parts).T
    q_inner = grad_q * my_gain
    p_inner = grad_p * my_gain
    final = jnp.concatenate(
        [jnp.sum(q_inner * q_normed, axis=1), jnp.sum(p_inner * p_normed, axis=1), last]
    )
    final = lax.all_gather(final, "group", axis=0)
    means = jnp.sum(final[:, : 2 * rows], axis=0) / width
    q_mean, p_mean = means[:rows, None], means[rows:, None]
    grad_queries = (q_inverse * (q_inner - q_normed * q_mean)).astype(BF16)
    grad_passages = (p_inverse * (p_inner - p_normed * p_mean)).astype(BF16)
    count = rows * n_data
    grad_gain = final[:, 2 * rows : 2 * rows + piece].reshape(-1) / math.sqrt(count)
    loss = final[0, 2 * rows + piece] / count
    return grad_queries, grad_passages, grad_gain, loss


def solution(mesh):
    nx = 4
    return jax.shard_map(
        functools.partial(local, nx),
        mesh=mesh,
        in_specs=(P("dp", "group"), P("dp", "group"), P("dp", None), P("dp", None), P()),
        out_specs=(P("dp", "group"), P("dp", "group"), P(), P()),
        check_vma=False,
    )
```
